512 devices in a mesh: slab: 16 (over y, core), plane: 32 (over x, z).
Axes of the slice: x: 4, y: 8, z: 8, core: 2. Of those that a mesh axis runs over, the one named last changes fastest.
Arguments:
- features: float32 [32, 48, 128, 1024], P(None, 'slab', 'plane'), may hold values from -6 to 6
- x_taps: float32 [32, 31], replicated, may hold values from -1 to 1
- y_taps: float32 [32, 31], replicated, may hold values from -1 to 1
- expand: bfloat16 [128, 32], replicated, may hold values from -1 to 1
- expand_bias: float32 [128], replicated, may hold values from -4 to 4
- project: bfloat16 [32, 128], replicated, may hold values from -0.5 to 0.5
- atlas_tiles: bfloat16 [128, 32, 2048], P('slab'), may hold values from -6 to 6
- footprint: int32 [16, 32], P('slab'), may hold values from -1 to 127, as said below
- block_slot: int32 [48, 128, 2], P('slab', 'plane'), may hold values from 0 to 31, as said below
- tile_base: int32 [3, 48, 128, 2], P(None, 'slab', 'plane'), may hold values from 0 to 7, as said below
- displacement: float32 [3, 48, 128, 1024], P(None, 'slab', 'plane'), may hold values from -1 to 9
Outputs:
- output: float32 [32, 48, 128, 1024], P(None, 'slab', 'plane')
The draws below stay inside these ranges and needn't reach their ends.
Inputs may be any that keep to these rules, and one draw needn't show every extreme that they name: `footprint`: entry o * 2 + k of row g is -1 or an atlas tile owned by slab group o, a number from o * 8 to (o + 1) * 8 - 1; within each aligned block of 2 entries the -1 entries come last; entries g * 2 to (g + 1) * 2 - 1 of row g are never -1. `block_slot`: each block names an entry of its slab group's row of footprint that is not -1. `tile_base`: component 0 is below 4; components 1 and 2 are below 8.
All inputs are finite; a program needn't handle non-finite values.
Results may differ from the reference program's by a relative error of at most 0.0027.
Values may be sent and summed in bfloat16 or wider, within the bound.
A program may use at most 128 MiB of HBM per device.

```python
import jax
import jax.numpy as jnp
from jax import lax

C = 32
HID = 128
KW = 31
X = 1024
ZD = 3
TZ = 8
TY = 16
TX = 16
BLK = 512
TILE_GRP = 8
CAP = 2
PV = 2048
NBX = 2
NT = 128
NZ = 48
NY = 128
N_SLAB = 16


def footprint_table(key):
    base_key = jax.random.fold_in(key, 11)
    count_key, order_key = jax.random.split(base_key)
    owners = jnp.arange(N_SLAB, dtype=jnp.int32)
    counts = jax.random.randint(count_key, (N_SLAB, N_SLAB), 0, CAP + 1)
    same = owners[:, None] == owners[None, :]
    following = (owners[:, None] + 1) % N_SLAB == owners[None, :]
    counts = jnp.where(same, CAP, counts)
    counts = jnp.where(following, CAP, counts)
    counts = counts.at[0, N_SLAB - 1].set(jnp.maximum(counts[0, N_SLAB - 1], 1))
    scores = jax.random.randint(order_key, (N_SLAB, N_SLAB, TILE_GRP), 0, 1 << 20) * TILE_GRP + jnp.arange(TILE_GRP, dtype=jnp.int32)
    ordering = jnp.argsort(scores, axis=2, stable=True).astype(jnp.int32)
    chosen = ordering[:, :, :CAP]
    rotated = (chosen - chosen[:, :, :1] + (TILE_GRP - 1)) % TILE_GRP
    chosen = jnp.where(following[:, :, None], rotated, chosen)
    chosen = chosen.at[0, N_SLAB - 1, 0].set(TILE_GRP - 1)
    tile_ids = owners[None, :, None] * TILE_GRP + chosen
    live = jnp.arange(CAP, dtype=jnp.int32)[None, None, :] < counts[:, :, None]
    table = jnp.where(live, tile_ids, -1).reshape(N_SLAB, N_SLAB * CAP)
    return (table.astype(jnp.int32), live.reshape(N_SLAB, N_SLAB * CAP))


def draw_footprint(key, part):
    table, live = footprint_table(key)
    return table


def draw_block_slot(key, part):
    table, live = footprint_table(key)
    live_count = live.astype(jnp.int32)
    totals = jnp.sum(live_count, axis=1)
    running = jnp.cumsum(live_count, axis=1)
    groups = jnp.arange(NZ, dtype=jnp.int32) // ZD
    picks = jax.random.randint(jax.random.fold_in(key, 12), (NZ, NY, NBX), 0, 1 << 20)
    ranks = picks % totals[groups][:, None, None]
    slots = jnp.sum((running[groups][:, None, None, :] <= ranks[..., None]).astype(jnp.int32), axis=3)
    first_plane = jnp.arange(NZ, dtype=jnp.int32) % ZD == 0
    next_slot = (groups + 1) % N_SLAB * CAP
    slots = slots.at[:, 1, 0].set(jnp.where(first_plane, next_slot, slots[:, 1, 0]))
    slots = slots.at[0, 0, 0].set(0)
    slots = slots.at[NZ - 1, NY - 1, NBX - 1].set(N_SLAB * CAP - 1)
    return slots.astype(jnp.int32)


def draw_tile_base(key, part):
    limits = jnp.array([TZ // 2, TY // 2, TX // 2], dtype=jnp.int32)
    picks = jax.random.randint(jax.random.fold_in(key, 13), (3, NZ, NY, NBX), 0, 1 << 20)
    bases = picks % limits[:, None, None, None]
    bases = bases.at[1, 0, 0, 0].set(TY // 2 - 1)
    bases = bases.at[0, 0, 0, 0].set(0)
    return bases.astype(jnp.int32)


def block_levels(own_key, dims, cuts, smallest, high):
    def one(dim, shards_of):
        steps = jax.random.uniform(jax.random.fold_in(jax.random.fold_in(own_key, 6), dim), (shards_of,), jnp.float32, smallest / len(cuts), high / len(cuts))
        return jnp.repeat(jnp.exp(steps), dims[dim] // shards_of).reshape((-1,) + (1,) * (len(dims) - dim - 1))

    factor_of = one(*cuts[0])
    for cut in cuts[1:]:
        factor_of = factor_of * one(*cut)
    return factor_of


def noise(own_key, dims, deviation, reach, shards=(), kind=jnp.bfloat16):
    values = deviation * jax.random.normal(own_key, dims, jnp.float32)
    if shards:
        values = values * block_levels(own_key, dims, shards, -0.22, 0.18)
    return jnp.clip(values, -reach, reach).astype(kind)


def setup_inputs(seed: int = 0) -> dict:
    key_of = jax.random.split(jax.random.key(seed), 12)
    features = noise(key_of[0], (C, NZ, NY, X), 1.0, 6.0, ((1, 16), (2, 32)), jnp.float32)
    x_taps = noise(key_of[1], (C, KW), KW ** -0.5, 1.0, (), jnp.float32)
    y_taps = noise(key_of[2], (C, KW), KW ** -0.5, 1.0, (), jnp.float32)
    expand = noise(key_of[3], (HID, C), C ** -0.5, 1.0)
    expand_bias = noise(key_of[4], (HID,), 1.0, 4.0, (), jnp.float32)
    project = noise(key_of[5], (C, HID), HID ** -0.5, 0.5)
    atlas_tiles = noise(key_of[6], (NT, C, PV), 1.0, 6.0, ((0, 16),))
    footprint = draw_footprint(jax.random.fold_in(key_of[11], 71), 0)
    block_slot = draw_block_slot(jax.random.fold_in(key_of[11], 71), 0)
    tile_base = draw_tile_base(jax.random.fold_in(key_of[11], 71), 0)
    displacement = jnp.clip(-1.0 + 10.0 * jax.random.uniform(key_of[10], (3, NZ, NY, X), jnp.float32) ** block_levels(key_of[10], (3, NZ, NY, X), ((1, 16), (2, 32)), -0.2, 0.2), -1.0, 9.0)
    return {"features": features, "x_taps": x_taps, "y_taps": y_taps, "expand": expand, "expand_bias": expand_bias, "project": project, "atlas_tiles": atlas_tiles, "footprint": footprint, "block_slot": block_slot, "tile_base": tile_base, "displacement": displacement}


def gelu_tanh(values):
    return 0.5 * values * (1.0 + jnp.tanh(0.7978845608028654 * (values + 0.044715 * values * values * values)))


def depthwise(field, taps, axis):
    half_taps = taps.shape[1] // 2
    padding = [(0, 0)] * field.ndim
    padding[axis] = (half_taps, half_taps)
    padded = jnp.pad(field, padding)
    length = field.shape[axis]
    total = jnp.zeros_like(field)
    for offset in range(taps.shape[1]):
        window = lax.slice_in_dim(padded, offset, offset + length, axis=axis)
        total = total + taps[:, offset].reshape((-1,) + (1,) * (field.ndim - 1)) * window
    return total


def tent(position, index):
    return jnp.maximum(0.0, 1.0 - jnp.abs(position - index))


def reference(features, x_taps, y_taps, expand, expand_bias, project, atlas_tiles, footprint, block_slot, tile_base, displacement):
    limits = (TZ, TY, TX)

    def group_block(group):
        start = group * ZD
        feats = lax.dynamic_slice_in_dim(features, start, ZD, 1)
        xconv = depthwise(feats, x_taps, 3)
        yconv = depthwise(xconv, y_taps, 2)
        mixed_in = yconv.astype(jnp.bfloat16).reshape(C, -1)
        hidden = gelu_tanh(jnp.dot(expand, mixed_in, preferred_element_type=jnp.float32) + expand_bias[:, None]).astype(jnp.bfloat16)
        mlp_out = jnp.dot(project, hidden, preferred_element_type=jnp.float32).reshape(feats.shape)
        shifts = lax.dynamic_slice_in_dim(displacement, start, ZD, 1).reshape(3, ZD * NY * NBX, BLK)
        bases = lax.dynamic_slice_in_dim(tile_base, start, ZD, 1).reshape(3, ZD * NY * NBX, 1).astype(jnp.float32)
        slots = lax.dynamic_slice_in_dim(block_slot, start, ZD, 0).reshape(-1)
        row_ids = lax.dynamic_index_in_dim(footprint, group, 0, keepdims=False)
        tile_ids = row_ids[slots].astype(jnp.int32)
        tiles = atlas_tiles[tile_ids]
        positions = bases + shifts
        corner_lists = []
        for axis_index in range(3):
            place = jnp.clip(positions[axis_index], 0.0, limits[axis_index] - 1.0)
            lower = jnp.minimum(jnp.floor(place), limits[axis_index] - 2.0)
            upper = lower + 1.0
            corner_lists.append([(lower.astype(jnp.int32), tent(place, lower)), (upper.astype(jnp.int32), tent(place, upper))])
        total = jnp.zeros((tiles.shape[0], C, BLK), jnp.float32)
        for corner_z in corner_lists[0]:
            for corner_y in corner_lists[1]:
                for corner_x in corner_lists[2]:
                    flat = corner_z[0] * (TY * TX) + corner_y[0] * TX + corner_x[0]
                    weight = ((corner_z[1] * corner_y[1]) * corner_x[1]).astype(jnp.bfloat16)
                    values = jnp.take_along_axis(tiles, flat[:, None, :], axis=2)
                    total = total + values.astype(jnp.float32) * weight.astype(jnp.float32)[:, None, :]
        warped = total.reshape(ZD, NY, NBX, C, BLK).transpose(3, 0, 1, 2, 4).reshape(C, ZD, NY, X)
        return (feats + mlp_out) + warped

    pieces = lax.map(group_block, jnp.arange(N_SLAB, dtype=jnp.int32))
    return pieces.transpose(1, 0, 2, 3, 4).reshape(C, NZ, NY, X)
```

```python
import functools

import jax
import jax.numpy as jnp
from jax import lax
from jax.experimental import pallas as pl
from jax.experimental.pallas import tpu as pltpu
from jax.sharding import PartitionSpec as P

TZ = 8
TY = 16
TX = 16
BLK = 512
KZ = 8
KX = 4
NP = KX * KZ
NS = 16
CAP = 2
SLOTS = NS * CAP
HELD = 8
ZD = 3
YR = 4
XQ = 4
QW = 256
ROWS = XQ * YR
F32 = jnp.float32
BF16 = jnp.bfloat16
MESH = pl.DeviceIdType.MESH


def dot(a, b):
    return jnp.dot(a, b, preferred_element_type=F32)


def split2(value):
    high = value.astype(BF16)
    return high, (value - high.astype(F32)).astype(BF16)


def exchange_kernel(
    feat_ref,
    xt_ref,
    yt_ref,
    fp_ref,
    atlas_ref,
    mixed_ref,
    lib_ref,
    feat,
    chunks,
    cols,
    back,
    pieces,
    picked,
    bm,
    tx,
    in_sem,
    a_send,
    a_recv,
    b_send,
    b_recv,
    b_own,
    y_send,
    y_recv,
    g_own,
    g_send,
    g_recv,
):
    s = lax.axis_index("slab")
    p = lax.axis_index("plane")
    px = p // KZ
    pz = lax.rem(p, KZ)

    loads = [
        pltpu.make_async_copy(feat_ref.at[:, z], feat.at[z], in_sem.at[z]) for z in range(ZD)
    ]
    half = p // 16
    cell = lax.rem(p, 16)
    atlas_load = pltpu.make_async_copy(
        atlas_ref.at[:, pl.ds(half * 16, 16), pl.ds(pl.multiple_of(cell * 128, 128), 128)],
        pieces.at[pl.ds(s * HELD, HELD)],
        in_sem.at[ZD],
    )
    atlas_load.start()
    for load in loads:
        load.start()

    barrier = pltpu.get_barrier_semaphore()

    def greet_plane(i, carry):
        pl.semaphore_signal(
            barrier, inc=1, device_id={"plane": lax.rem(p + i, NP)}, device_id_type=MESH
        )
        return carry

    def greet_slab(i, carry):
        pl.semaphore_signal(
            barrier, inc=1, device_id={"slab": lax.rem(s + i, NS)}, device_id_type=MESH
        )
        return carry

    lax.fori_loop(1, NP, greet_plane, 0)
    lax.fori_loop(1, NS, greet_slab, 0)

    def make_chunks(z):
        loads[z].wait()

        def step(c, carry):
            block = feat[z, c]
            stacked = jnp.concatenate(
                [block[:, q * QW : (q + 1) * QW] for q in range(XQ)], axis=0
            )
            chunks[z, c] = stacked.astype(BF16)
            return carry

        lax.fori_loop(0, NP, step, 0)

    def send_chunks(z):
        def step(i, carry):
            peer = lax.rem(p + i, NP)
            pltpu.make_async_remote_copy(
                chunks.at[z, peer],
                cols.at[z, p],
                a_send.at[z],
                a_recv.at[z],
                device_id={"plane": peer},
                device_id_type=MESH,
            ).start()
            return carry

        lax.fori_loop(1, NP, step, 0)
        cols[z, p] = chunks[z, p]

    make_chunks(0)
    atlas_load.wait()
    pl.semaphore_wait(barrier, NP - 1 + NS - 1)

    def send_piece(i, carry):
        peer = lax.rem(s + i, NS)
        pltpu.make_async_remote_copy(
            pieces.at[pl.ds(s * HELD, HELD)],
            pieces.at[pl.ds(s * HELD, HELD)],
            y_send,
            y_recv,
            device_id={"slab": peer},
            device_id_type=MESH,
        ).start()
        return carry

    lax.fori_loop(1, NS, send_piece, 0)
    send_chunks(0)
    for z in range(1, ZD):
        make_chunks(z)
        send_chunks(z)

    size = NP * ROWS

    def taps_at(index, ref):
        total = jnp.zeros(index.shape, F32)
        for t in range(31):
            total = jnp.where(index == t, ref[p, t], total)
        return total

    def build_rows(m, carry):
        out = lax.broadcasted_iota(jnp.int32, (64, size), 0) + m * 64
        inp = lax.broadcasted_iota(jnp.int32, (64, size), 1)
        row = lambda r: lax.shift_right_logical(r, 4) * 4 + (r & 3)
        quarter = lambda r: lax.shift_right_logical(r, 2) & 3
        weights = taps_at(row(inp) - row(out) + 15, yt_ref)
        for n, shift in enumerate((0, -1, 1)):
            kept = jnp.where(quarter(inp) == quarter(out) + shift, weights, 0.0)
            high, low = split2(kept)
            bm[2 * n, pl.ds(m * 64, 64)] = high
            bm[2 * n + 1, pl.ds(m * 64, 64)] = low
        return carry

    lax.fori_loop(0, size // 64, build_rows, 0)

    def build_x(m, carry):
        k = lax.broadcasted_iota(jnp.int32, (64, QW), 0) + m * 64
        n = lax.broadcasted_iota(jnp.int32, (64, QW), 1)
        high, low = split2(taps_at(k - 128 - n + 15, xt_ref))
        tx[0, pl.ds(m * 64, 64)] = high
        tx[1, pl.ds(m * 64, 64)] = low
        return carry

    lax.fori_loop(0, 8, build_x, 0)

    wait_all = lambda ref, sem: pltpu.make_async_copy(ref, ref, sem).wait()
    wait_all(pieces.at[pl.ds(0, (NS - 1) * HELD)], y_recv)

    def pick(slot, carry):
        tile = jnp.maximum(fp_ref[0, slot], 0)
        picked[slot] = pieces[tile]
        return carry

    lax.fori_loop(0, SLOTS, pick, 0)

    sends = []

    def pass_on(source, target, count, device, sem, index):
        copy = pltpu.make_async_remote_copy(
            source,
            target,
            g_send.at[len(sends)],
            g_recv.at[index],
            device_id={"plane": device},
            device_id_type=MESH,
        )
        copy.start()
        sends.append(copy)
        return copy

    at = lambda x, z: lax.rem(x + KX, KX) * KZ + lax.rem(z + KZ, KZ)
    up, down = at(px, pz + 1), at(px, pz - 1)
    right, left = at(px + 1, pz), at(px - 1, pz)
    first, second = pl.ds(0, SLOTS // 2), pl.ds(SLOTS // 2, SLOTS // 2)
    recv = {}

    def spread(dz, source, target):
        index = dz + 3
        recv["r", dz] = pass_on(source, target, SLOTS, right, g_recv, 7 + index)
        recv["l", dz] = pass_on(source, target, SLOTS, left, g_recv, 15 + index)

    own = lib_ref.at[p]
    recv["u", 1] = pass_on(picked, own, SLOTS, up, g_recv, 0)
    recv["d", 1] = pass_on(picked, own, SLOTS, down, g_recv, 4)
    spread(0, picked, own)
    own_copy = pltpu.make_async_copy(picked, own, g_own)
    own_copy.start()

    def z_step(r):
        recv["u", r].wait_recv()
        piece = lib_ref.at[at(px, pz - r)]
        if r < 4:
            recv["u", r + 1] = pass_on(piece, piece, SLOTS, up, g_recv, r)
        spread(-r if r < 4 else 4, piece, piece)
        if r < 4:
            recv["d", r].wait_recv()
            piece = lib_ref.at[at(px, pz + r)]
            if r < 3:
                recv["d", r + 1] = pass_on(piece, piece, SLOTS, down, g_recv, 4 + r)
            spread(r, piece, piece)

    def x_step(dz):
        index = dz + 3
        recv["r", dz].wait_recv()
        piece = lib_ref.at[at(px - 1, pz + dz), first]
        recv["rr", dz] = pass_on(piece, piece, SLOTS // 2, right, g_recv, 23 + index)
        recv["l", dz].wait_recv()
        piece = lib_ref.at[at(px + 1, pz + dz), second]
        recv["ll", dz] = pass_on(piece, piece, SLOTS // 2, left, g_recv, 31 + index)

    def convolve(z):
        wait_all(cols.at[z, pl.ds(0, NP - 1)], a_recv.at[z])

        def step(m, carry):
            rows = pl.ds(m * 128, 128)
            x = cols[z].reshape(size, QW)
            main = dot(bm[0, rows], x) + dot(bm[1, rows], x)
            before = dot(bm[2, rows], x[:, 128:]) + dot(bm[3, rows], x[:, 128:])
            after = dot(bm[4, rows], x[:, :128]) + dot(bm[5, rows], x[:, :128])
            high, low = split2(jnp.concatenate([before, main, after], axis=1))
            out = dot(high, tx[0]) + dot(low, tx[0]) + dot(high, tx[1])
            back[z, pl.ds(m * 8, 8)] = out.astype(BF16).reshape(8, ROWS, QW)
            return carry

        lax.fori_loop(0, size // 128, step, 0)

        def send(i, carry):
            peer = lax.rem(p + i, NP)
            pltpu.make_async_remote_copy(
                back.at[z, peer],
                mixed_ref.at[z, p],
                b_send.at[z],
                b_recv.at[z],
                device_id={"plane": peer},
                device_id_type=MESH,
            ).start()
            return carry

        lax.fori_loop(1, NP, send, 0)
        own_back = pltpu.make_async_copy(back.at[z, p], mixed_ref.at[z, p], b_own.at[z])
        own_back.start()
        return own_back

    owns = []
    z_step(1)
    owns.append(convolve(0))
    x_step(0)
    z_step(2)
    x_step(-1)
    x_step(1)
    owns.append(convolve(1))
    z_step(3)
    x_step(-2)
    x_step(2)
    owns.append(convolve(2))
    z_step(4)
    x_step(-3)
    x_step(3)
    x_step(4)

    for dz in range(-3, 5):
        recv["rr", dz].wait_recv()
        recv["ll", dz].wait_recv()
    for copy in sends:
        copy.wait_send()
    own_copy.wait()
    wait_all(pieces.at[pl.ds(0, (NS - 1) * HELD)], y_send)
    for z in range(ZD):
        wait_all(chunks.at[z, pl.ds(0, NP - 1)], a_send.at[z])
        wait_all(back.at[z, pl.ds(0, NP - 1)], b_send.at[z])
        pltpu.make_async_copy(
            mixed_ref.at[z, pl.ds(0, NP - 1)], mixed_ref.at[z, pl.ds(0, NP - 1)], b_recv.at[z]
        ).wait()
        owns[z].wait()


def exchange(features, x_taps, y_taps, footprint, atlas_tiles):
    size = NP * ROWS
    anywhere = pl.BlockSpec(memory_space=pl.ANY)
    scalars = pl.BlockSpec(memory_space=pltpu.SMEM)
    dma = pltpu.SemaphoreType.DMA
    return pl.pallas_call(
        exchange_kernel,
        out_shape=(
            jax.ShapeDtypeStruct((ZD, NP, ROWS, QW), BF16),
            jax.ShapeDtypeStruct((NP, SLOTS, 16, 128), BF16),
        ),
        in_specs=[anywhere, scalars, scalars, scalars, anywhere],
        out_specs=(anywhere, anywhere),
        scratch_shapes=[
            pltpu.VMEM((ZD, NP, YR, XQ * QW), F32),
            pltpu.VMEM((ZD, NP, ROWS, QW), BF16),
            pltpu.VMEM((ZD, NP, ROWS, QW), BF16),
            pltpu.VMEM((ZD, NP, ROWS, QW), BF16),
            pltpu.VMEM((NS * HELD, 16, 128), BF16),
            pltpu.VMEM((SLOTS, 16, 128), BF16),
            pltpu.VMEM((6, size, size), BF16),
            pltpu.VMEM((2, 2 * QW, QW), BF16),
            dma((ZD + 1,)),
            dma((ZD,)),
            dma((ZD,)),
            dma((ZD,)),
            dma((ZD,)),
            dma((ZD,)),
            dma(()),
            dma(()),
            dma(()),
            dma((39,)),
            dma((39,)),
        ],
        compiler_params=pltpu.CompilerParams(
            collective_id=0, has_side_effects=True, vmem_limit_bytes=40 * 1024 * 1024
        ),
        cost_estimate=pl.CostEstimate(flops=6_000_000_000, bytes_accessed=10_000_000, transcendentals=0),
    )(features, x_taps, y_taps, footprint, atlas_tiles)


def gelu(a):
    inner = a * (0.7978845608028654 + (0.7978845608028654 * 0.044715) * (a * a))
    half = 0.5 * a
    return half + half * jnp.tanh(inner)


def combine_kernel(
    slot_ref,
    base_ref,
    feat_ref,
    mixed_ref,
    lib_ref,
    disp_ref,
    expand_ref,
    bias_ref,
    project_ref,
    out_ref,
    em,
    bias,
    wzy,
    rows_out,
):
    z = pl.program_id(0)
    hid = expand_ref.shape[0]

    @pl.when(z == 0)
    def _():
        lane = lax.broadcasted_iota(jnp.int32, expand_ref.shape, 1) & (ROWS - 1)

        def mask(r, carry):
            em[r] = jnp.where(lane == r, expand_ref[...].astype(F32), 0.0).astype(BF16)
            return carry

        lax.fori_loop(0, ROWS, mask, 0)
        bias[...] = jnp.broadcast_to(bias_ref[...], (hid, QW))

    def tent(place, cells):
        grid = lax.broadcasted_iota(jnp.int32, (cells, BLK), 0).astype(F32)
        return jnp.maximum(0.0, 1.0 - jnp.abs(place - grid))

    def block(n, carry):
        y = n // 2
        xh = lax.rem(n, 2)
        lanes = pl.ds(pl.multiple_of(xh * BLK, BLK), BLK)

        def place(axis, cells):
            base = base_ref[axis, z, y, xh].astype(F32)
            return jnp.clip(disp_ref[axis, 0, pl.ds(y, 1), lanes] + base, 0.0, cells - 1.0)

        wz = tent(place(0, TZ), TZ)
        wy = tent(place(1, TY), TY)
        wx = tent(place(2, TX), TX)
        for i in range(TZ):
            wzy[i * TY : (i + 1) * TY] = wz[i : i + 1] * wy
        slot = slot_ref[z, y, xh]
        total = jnp.zeros((NP, BLK), F32)
        for i in range(TZ):
            interp = jnp.concatenate(
                [(wzy[i * TY + j : i * TY + j + 1] * wx).astype(BF16) for j in range(TY)], axis=0
            )
            tile = jnp.concatenate(
                [
                    jnp.concatenate([lib_ref[16 * h + 2 * i + k, slot] for k in range(2)], axis=1)
                    for h in range(2)
                ],
                axis=0,
            )
            total = total + dot(tile, interp)
        parts = []
        for k in range(2):
            hidden = dot(em[xh * 8 + k * 4 + y], mixed_ref[0]) + bias[...]
            parts.append(dot(project_ref[...], gelu(hidden).astype(BF16)))
        total = total + jnp.concatenate(parts, axis=1)
        for k in range(BLK // 128):
            rows_out[xh * 4 + k, pl.ds(y, NP, stride=YR)] = total[:, k * 128 : (k + 1) * 128]
        return carry

    lax.fori_loop(0, YR * 2, block, 0)

    def write(g, carry):
        rows = pl.ds(pl.multiple_of(g * 8, 8), 8)
        two = jnp.concatenate([rows_out[k, rows] for k in range(8)], axis=1)
        out_ref[pl.ds(g * 2, 2), 0] = feat_ref[pl.ds(g * 2, 2), 0] + two.reshape(2, YR, XQ * QW)
        return carry

    lax.fori_loop(0, NP // 2, write, 0)


def combine(features, mixed, library, block_slot, tile_base, displacement, expand, expand_bias, project):
    hid = expand.shape[0]
    spread = jnp.repeat(expand, ROWS, axis=1)
    scalars = pl.BlockSpec(memory_space=pltpu.SMEM)
    whole = lambda *shape: pl.BlockSpec(shape, lambda z: (0,) * len(shape))
    return pl.pallas_call(
        combine_kernel,
        grid=(ZD,),
        out_shape=jax.ShapeDtypeStruct(features.shape, F32),
        in_specs=[
            scalars,
            scalars,
            pl.BlockSpec((NP, 1, YR, XQ * QW), lambda z: (0, z, 0, 0)),
            pl.BlockSpec((1, NP * ROWS, QW), lambda z: (z, 0, 0)),
            whole(NP, SLOTS, 16, 128),
            pl.BlockSpec((3, 1, YR, XQ * QW), lambda z: (0, z, 0, 0)),
            whole(hid, NP * ROWS),
            whole(hid, 1),
            whole(NP, hid),
        ],
        out_specs=pl.BlockSpec((NP, 1, YR, XQ * QW), lambda z: (0, z, 0, 0)),
        scratch_shapes=[
            pltpu.VMEM((ROWS, hid, NP * ROWS), BF16),
            pltpu.VMEM((hid, QW), F32),
            pltpu.VMEM((TZ * TY, BLK), F32),
            pltpu.VMEM((8, NP * YR, 128), F32),
        ],
        compiler_params=pltpu.CompilerParams(vmem_limit_bytes=40 * 1024 * 1024),
        cost_estimate=pl.CostEstimate(
            flops=4_000_000_000, bytes_accessed=10_000_000, transcendentals=1_600_000
        ),
    )(
        block_slot,
        tile_base,
        features,
        mixed.reshape(ZD, NP * ROWS, QW),
        library,
        displacement,
        spread,
        expand_bias.reshape(hid, 1),
        project,
    )


def body(
    features,
    x_taps,
    y_taps,
    expand,
    expand_bias,
    project,
    atlas_tiles,
    footprint,
    block_slot,
    tile_base,
    displacement,
):
    mixed, library = exchange(features, x_taps, y_taps, footprint, atlas_tiles)
    return combine(
        features, mixed, library, block_slot, tile_base, displacement, expand, expand_bias, project
    )


def solution(mesh):
    return jax.shard_map(
        body,
        mesh=mesh,
        in_specs=(
            P(None, "slab", "plane", None),
            P(),
            P(),
            P(),
            P(),
            P(),
            P("slab", None, None),
            P("slab", None),
            P("slab", "plane", None),
            P(None, "slab", "plane", None),
            P(None, "slab", "plane", None),
        ),
        out_specs=P(None, "slab", "plane", None),
        check_vma=False,
    )
```

```python
import functools

import jax
import jax.numpy as jnp
from jax import lax
from jax.experimental import pallas as pl
from jax.experimental.pallas import tpu as pltpu
from jax.sharding import PartitionSpec as P

TZ = 8
TY = 16
TX = 16
BLK = 512
KZ = 8
KX = 4
NP = KX * KZ
NS = 16
CAP = 2
SLOTS = NS * CAP
HELD = 8
ZD = 3
YR = 4
XQ = 4
QW = 256
ROWS = XQ * YR
NB = ZD * YR * 2
GROUPS = tuple(range(-3, 5))
F32 = jnp.float32
BF16 = jnp.bfloat16
MESH = pl.DeviceIdType.MESH


def dot(a, b):
    return jnp.dot(a, b, preferred_element_type=F32)


def split2(value):
    high = value.astype(BF16)
    return high, (value - high.astype(F32)).astype(BF16)


def gelu(a):
    inner = a * (0.7978845608028654 + (0.7978845608028654 * 0.044715) * (a * a))
    half = 0.5 * a
    return half + half * jnp.tanh(inner)


def wait_all(ref, sem):
    pltpu.make_async_copy(ref, ref, sem).wait()


def block_kernel(
    feat_ref,
    xt_ref,
    yt_ref,
    expand_ref,
    bias_ref,
    project_ref,
    atlas_ref,
    fp_ref,
    slot_ref,
    base_ref,
    disp_ref,
    out_ref,
    feat,
    chunks,
    cols,
    back,
    mixed,
    pieces,
    picked,
    lib,
    bm,
    tx,
    expand,
    bias,
    wx_all,
    wy_all,
    pz_all,
    wzy,
    acc,
    wide,
    rows_out,
    in_sem,
    a_send,
    a_recv,
    b_send,
    b_recv,
    b_own,
    y_send,
    y_recv,
    g_own,
    g_send,
    g_recv,
):
    s = lax.axis_index("slab")
    p = lax.axis_index("plane")
    px = p // KZ
    pz = lax.rem(p, KZ)
    hid = project_ref.shape[1]
    size = NP * ROWS
    lib = dict(zip(GROUPS, lib))

    barrier = pltpu.get_barrier_semaphore()

    def greet_plane(i, carry):
        pl.semaphore_signal(
            barrier, inc=1, device_id={"plane": lax.rem(p + i, NP)}, device_id_type=MESH
        )
        return carry

    def greet_slab(i, carry):
        pl.semaphore_signal(
            barrier, inc=1, device_id={"slab": lax.rem(s + i, NS)}, device_id_type=MESH
        )
        return carry

    lax.fori_loop(1, NP, greet_plane, 0)
    lax.fori_loop(1, NS, greet_slab, 0)

    loads = [
        pltpu.make_async_copy(feat_ref.at[:, z], feat.at[z], in_sem.at[z]) for z in range(ZD)
    ]
    half = px // 2
    cell = 2 * pz + lax.rem(px, 2)
    atlas_load = pltpu.make_async_copy(
        atlas_ref.at[
            :,
            pl.ds(pl.multiple_of(half * 16, 16), 16),
            pl.ds(pl.multiple_of(cell * 128, 128), 128),
        ],
        pieces.at[pl.ds(s * HELD, HELD)],
        in_sem.at[ZD],
    )
    atlas_load.start()
    for load in loads:
        load.start()

    def make_chunks(z):
        loads[z].wait()

        def step(c, carry):
            block = feat[z, c]
            stacked = jnp.concatenate(
                [block[:, q * QW : (q + 1) * QW] for q in range(XQ)], axis=0
            )
            chunks[z, c] = stacked.astype(BF16)
            return carry

        lax.fori_loop(0, NP, step, 0)

    def send_chunks(z):
        def step(i, carry):
            peer = lax.rem(p + i, NP)
            pltpu.make_async_remote_copy(
                chunks.at[z, peer],
                cols.at[z, p],
                a_send.at[z],
                a_recv.at[z],
                device_id={"plane": peer},
                device_id_type=MESH,
            ).start()
            return carry

        lax.fori_loop(1, NP, step, 0)

    for z in range(ZD):
        make_chunks(z)
        cols[z, p] = chunks[z, p]
    atlas_load.wait()
    pl.semaphore_wait(barrier, NP - 1 + NS - 1)

    def send_piece(i, carry):
        peer = lax.rem(s + i, NS)
        pltpu.make_async_remote_copy(
            pieces.at[pl.ds(s * HELD, HELD)],
            pieces.at[pl.ds(s * HELD, HELD)],
            y_send,
            y_recv,
            device_id={"slab": peer},
            device_id_type=MESH,
        ).start()
        return carry

    lax.fori_loop(1, NS, send_piece, 0)
    for z in range(ZD):
        send_chunks(z)

    def taps_at(index, ref):
        total = jnp.zeros(index.shape, F32)
        for t in range(31):
            total = jnp.where(index == t, ref[p, t], total)
        return total

    def build_rows(m, carry):
        out = lax.broadcasted_iota(jnp.int32, (64, size), 0) + m * 64
        inp = lax.broadcasted_iota(jnp.int32, (64, size), 1)
        row = lambda r: lax.shift_right_logical(r, 4) * 4 + (r & 3)
        quarter = lambda r: lax.shift_right_logical(r, 2) & 3
        weights = taps_at(row(inp) - row(out) + 15, yt_ref)
        for n, shift in enumerate((0, -1, 1)):
            kept = jnp.where(quarter(inp) == quarter(out) + shift, weights, 0.0)
            high, low = split2(kept)
            bm[2 * n, pl.ds(m * 64, 64)] = high
            bm[2 * n + 1, pl.ds(m * 64, 64)] = low
        return carry

    lax.fori_loop(0, size // 64, build_rows, 0)

    def build_x(m, carry):
        k = lax.broadcasted_iota(jnp.int32, (64, QW), 0) + m * 64
        n = lax.broadcasted_iota(jnp.int32, (64, QW), 1)
        high, low = split2(taps_at(k - 128 - n + 15, xt_ref))
        tx[0, pl.ds(m * 64, 64)] = high
        tx[1, pl.ds(m * 64, 64)] = low
        return carry

    lax.fori_loop(0, 8, build_x, 0)

    expand[...] = jnp.transpose(expand_ref[...].astype(F32)).astype(BF16)
    bias[...] = jnp.transpose(jnp.broadcast_to(bias_ref[...], (hid, hid)))

    def tents(n, carry):
        z = n // 8
        y = lax.rem(n, 8) // 2
        xh = lax.rem(n, 2)
        lanes = pl.ds(pl.multiple_of(xh * BLK, BLK), BLK)

        def place(axis, cells):
            base = base_ref[axis, z, xh, y].astype(F32)
            return jnp.clip(disp_ref[axis, z, pl.ds(y, 1), lanes] + base, 0.0, cells - 1.0)

        def tent(axis, cells):
            grid = lax.broadcasted_iota(jnp.int32, (cells, BLK), 0).astype(F32)
            return jnp.maximum(0.0, 1.0 - jnp.abs(place(axis, cells) - grid))

        wy_all[n] = tent(1, TY)
        wx_all[n] = tent(2, TX)
        pz_all[n] = jnp.broadcast_to(place(0, TZ), (8, BLK))
        acc[n] = jnp.zeros((NP, BLK), F32)
        return carry

    lax.fori_loop(0, NB, tents, 0)

    sends = []

    def pass_on(source, target, device, index):
        copy = pltpu.make_async_remote_copy(
            source,
            target,
            g_send.at[len(sends)],
            g_recv.at[index],
            device_id={"plane": device},
            device_id_type=MESH,
        )
        copy.start()
        sends.append(copy)
        return copy

    at = lambda x, z: lax.rem(x + KX, KX) * KZ + lax.rem(z + KZ, KZ)
    column = lambda d: lax.rem(px + d + KX, KX)
    up, down = at(px, pz + 1), at(px, pz - 1)
    right, left = at(px + 1, pz), at(px - 1, pz)
    first, second = pl.ds(0, SLOTS // 2), pl.ds(SLOTS // 2, SLOTS // 2)
    recv = {}

    def spread(dz, source):
        target = lib[dz].at[px]
        recv["r", dz] = pass_on(source, target, right, 7 + dz + 3)
        recv["l", dz] = pass_on(source, target, left, 15 + dz + 3)

    def start_ring():
        wait_all(pieces.at[pl.ds(0, (NS - 1) * HELD)], y_recv)

        def pick(slot, carry):
            tile = jnp.maximum(fp_ref[0, slot], 0)
            picked[slot] = pieces[tile]
            return carry

        lax.fori_loop(0, SLOTS, pick, 0)
        recv["u", 1] = pass_on(picked, lib[-1].at[px], up, 0)
        recv["d", 1] = pass_on(picked, lib[1].at[px], down, 4)
        spread(0, picked)
        copy = pltpu.make_async_copy(picked, lib[0].at[px], g_own)
        copy.start()
        return copy

    def z_step(r):
        recv["u", r].wait_recv()
        dz = -r if r < 4 else 4
        piece = lib[dz].at[px]
        if r < 4:
            recv["u", r + 1] = pass_on(piece, lib[-r - 1 if r < 3 else 4].at[px], up, r)
        spread(dz, piece)
        if r < 4:
            recv["d", r].wait_recv()
            piece = lib[r].at[px]
            if r < 3:
                recv["d", r + 1] = pass_on(piece, lib[r + 1].at[px], down, 4 + r)
            spread(r, piece)

    def x_step(dz):
        recv["r", dz].wait_recv()
        piece = lib[dz].at[column(-1), first]
        recv["rr", dz] = pass_on(piece, piece, right, 23 + dz + 3)
        recv["l", dz].wait_recv()
        piece = lib[dz].at[column(1), second]
        recv["ll", dz] = pass_on(piece, piece, left, 31 + dz + 3)

    def sample(dz):
        recv["rr", dz].wait_recv()
        recv["ll", dz].wait_recv()
        index = lax.rem(pz + dz + KZ, KZ).astype(F32)

        def step(n, carry):
            slot = slot_ref[n // 8, lax.rem(n, 2), lax.rem(n, 8) // 2]
            wz = jnp.maximum(0.0, 1.0 - jnp.abs(pz_all[n] - index))
            wy = wy_all[n]
            wzy[0:8] = wz * wy[0:8]
            wzy[8:16] = wz * wy[8:16]
            wx = wx_all[n]
            interp = jnp.concatenate(
                [(wzy[j : j + 1] * wx).astype(BF16) for j in range(TY)], axis=0
            )
            tile = jnp.concatenate(
                [
                    jnp.concatenate([lib[dz][2 * h + k, slot] for k in range(2)], axis=1)
                    for h in range(2)
                ],
                axis=0,
            )
            acc[n] = acc[n] + dot(tile, interp)
            return carry

        lax.fori_loop(0, NB, step, 0)

    def convolve(z):
        wait_all(cols.at[z, pl.ds(0, NP - 1)], a_recv.at[z])

        def step(m, carry):
            rows = pl.ds(m * 256, 256)
            x = cols[z].reshape(size, QW)
            main = dot(bm[0, rows], x) + dot(bm[1, rows], x)
            before = dot(bm[2, rows], x[:, 128:]) + dot(bm[3, rows], x[:, 128:])
            after = dot(bm[4, rows], x[:, :128]) + dot(bm[5, rows], x[:, :128])
            high, low = split2(jnp.concatenate([before, main, after], axis=1))
            out = dot(high, tx[0]) + dot(low, tx[0]) + dot(high, tx[1])
            back[z, pl.ds(m * 16, 16)] = out.astype(BF16).reshape(16, ROWS, QW)
            return carry

        lax.fori_loop(0, size // 256, step, 0)

        def send(i, carry):
            peer = lax.rem(p + i, NP)
            pltpu.make_async_remote_copy(
                back.at[z, peer],
                mixed.at[z, p],
                b_send.at[z],
                b_recv.at[z],
                device_id={"plane": peer},
                device_id_type=MESH,
            ).start()
            return carry

        lax.fori_loop(1, NP, send, 0)
        own = pltpu.make_async_copy(back.at[z, p], mixed.at[z, p], b_own.at[z])
        own.start()
        return own

    def perceive(z, own):
        wait_all(mixed.at[z, pl.ds(0, NP - 1)], b_recv.at[z])
        own.wait()

        def widen(i, carry):
            two = mixed[z, pl.ds(i * 2, 2)].reshape(2 * ROWS, QW).astype(F32)
            for k in range(2):
                wide[k, pl.ds(pl.multiple_of(i * 32, 32), 32)] = two[:, k * 128 : (k + 1) * 128]
            return carry

        lax.fori_loop(0, NP // 2, widen, 0)

        def step(n, carry):
            y = n // 2
            xh = lax.rem(n, 2)
            x = jnp.concatenate(
                [
                    wide[l, pl.ds(8 * xh + 4 * k + y, NP, stride=ROWS)]
                    for k in range(2)
                    for l in range(2)
                ],
                axis=1,
            ).astype(BF16)
            b = bias[...]
            hidden = dot(expand[...], x) + jnp.concatenate([b] * 4, axis=1)
            acc[z * 8 + n] = acc[z * 8 + n] + dot(project_ref[...], gelu(hidden).astype(BF16))
            return carry

        lax.fori_loop(0, 8, step, 0)

    owns = [convolve(0)]
    own_copy = start_ring()
    owns.append(convolve(1))
    z_step(1)
    owns.append(convolve(2))
    x_step(0)
    z_step(2)
    x_step(-1)
    x_step(1)
    own_copy.wait()
    sample(0)
    z_step(3)
    x_step(-2)
    x_step(2)
    sample(-1)
    z_step(4)
    sample(1)
    x_step(-3)
    x_step(3)
    sample(-2)
    perceive(0, owns[0])
    x_step(4)
    sample(2)
    perceive(1, owns[1])
    sample(-3)
    sample(3)
    perceive(2, owns[2])
    sample(4)

    def finish(z, carry):
        def turn(n, carry):
            y = n // 2
            xh = lax.rem(n, 2)
            value = acc[z * 8 + n]
            for k in range(BLK // 128):
                rows_out[xh * 4 + k, pl.ds(y, NP, stride=YR)] = value[:, k * 128 : (k + 1) * 128]
            return carry

        lax.fori_loop(0, 8, turn, 0)

        def write(g, carry):
            rows = pl.ds(pl.multiple_of(g * 8, 8), 8)
            two = jnp.concatenate([rows_out[k, rows] for k in range(8)], axis=1)
            out_ref[pl.ds(g * 2, 2), z] = two.reshape(2, YR, XQ * QW)
            return carry

        lax.fori_loop(0, NP // 2, write, 0)
        return carry

    lax.fori_loop(0, ZD, finish, 0)

    for copy in sends:
        copy.wait_send()
    wait_all(pieces.at[pl.ds(0, (NS - 1) * HELD)], y_send)
    for z in range(ZD):
        wait_all(chunks.at[z, pl.ds(0, NP - 1)], a_send.at[z])
        wait_all(back.at[z, pl.ds(0, NP - 1)], b_send.at[z])


def body(
    features,
    x_taps,
    y_taps,
    expand,
    expand_bias,
    project,
    atlas_tiles,
    footprint,
    block_slot,
    tile_base,
    displacement,
):
    size = NP * ROWS
    hid = expand.shape[0]
    hbm = pl.BlockSpec(memory_space=pltpu.HBM)
    scalars = pl.BlockSpec(memory_space=pltpu.SMEM)
    vmem = pl.BlockSpec(memory_space=pltpu.VMEM)
    dma = pltpu.SemaphoreType.DMA
    added = pl.pallas_call(
        block_kernel,
        out_shape=jax.ShapeDtypeStruct(features.shape, F32),
        in_specs=[
            hbm,
            scalars,
            scalars,
            vmem,
            vmem,
            vmem,
            hbm,
            scalars,
            scalars,
            scalars,
            vmem,
        ],
        out_specs=vmem,
        scratch_shapes=[
            pltpu.VMEM((ZD, NP, YR, XQ * QW), F32),
            pltpu.VMEM((ZD, NP, ROWS, QW), BF16),
            pltpu.VMEM((ZD, NP, ROWS, QW), BF16),
            pltpu.VMEM((ZD, NP, ROWS, QW), BF16),
            pltpu.VMEM((ZD, NP, ROWS, QW), BF16),
            pltpu.VMEM((NS * HELD, 16, 128), BF16),
            pltpu.VMEM((SLOTS, 16, 128), BF16),
            [pltpu.VMEM((KX, SLOTS, 16, 128), BF16) for _ in GROUPS],
            pltpu.VMEM((6, size, size), BF16),
            pltpu.VMEM((2, 2 * QW, QW), BF16),
            pltpu.VMEM((hid, NP), BF16),
            pltpu.VMEM((hid, hid), F32),
            pltpu.VMEM((NB, TX, BLK), F32),
            pltpu.VMEM((NB, TY, BLK), F32),
            pltpu.VMEM((NB, 8, BLK), F32),
            pltpu.VMEM((TY, BLK), F32),
            pltpu.VMEM((NB, NP, BLK), F32),
            pltpu.VMEM((2, size, 128), F32),
            pltpu.VMEM((8, NP * YR, 128), F32),
            dma((ZD + 1,)),
            dma((ZD,)),
            dma((ZD,)),
            dma((ZD,)),
            dma((ZD,)),
            dma((ZD,)),
            dma(()),
            dma(()),
            dma(()),
            dma((39,)),
            dma((39,)),
        ],
        compiler_params=pltpu.CompilerParams(
            collective_id=0, has_side_effects=True, vmem_limit_bytes=48 * 1024 * 1024
        ),
        cost_estimate=pl.CostEstimate(
            flops=10_000_000_000, bytes_accessed=10_000_000, transcendentals=1_600_000
        ),
    )(
        features,
        x_taps,
        y_taps,
        expand.T,
        expand_bias.reshape(1, hid),
        project,
        atlas_tiles,
        footprint,
        jnp.swapaxes(block_slot, 1, 2),
        jnp.swapaxes(tile_base, 2, 3),
        displacement,
    )
    return features + added


def solution(mesh):
    return jax.shard_map(
        body,
        mesh=mesh,
        in_specs=(
            P(None, "slab", "plane", None),
            P(),
            P(),
            P(),
            P(),
            P(),
            P("slab", None, None),
            P("slab", None),
            P("slab", "plane", None),
            P(None, "slab", "plane", None),
            P(None, "slab", "plane", None),
        ),
        out_specs=P(None, "slab", "plane", None),
        check_vma=False,
    )
```

```python
import functools

import jax
import jax.numpy as jnp
from jax import lax
from jax.experimental import pallas as pl
from jax.experimental.pallas import tpu as pltpu
from jax.sharding import PartitionSpec as P

TZ = 8
TY = 16
TX = 16
BLK = 512
KZ = 8
KX = 4
NP = KX * KZ
NS = 16
KY = NS // 2
CAP = 2
SLOTS = NS * CAP
HELD = 8
ZD = 3
YR = 4
XQ = 4
QW = 256
ROWS = XQ * YR
NB = ZD * YR * 2
GROUPS = tuple(range(-3, 5))
F32 = jnp.float32
BF16 = jnp.bfloat16
MESH = pl.DeviceIdType.MESH


def dot(a, b):
    return jnp.dot(a, b, preferred_element_type=F32)


def split2(value):
    high = value.astype(BF16)
    return high, (value - high.astype(F32)).astype(BF16)


def gelu(a):
    inner = a * (0.7978845608028654 + (0.7978845608028654 * 0.044715) * (a * a))
    half = 0.5 * a
    return half + half * jnp.tanh(inner)


def wait_all(ref, sem):
    pltpu.make_async_copy(ref, ref, sem).wait()


def block_kernel(
    feat_ref,
    xt_ref,
    yt_ref,
    expand_ref,
    bias_ref,
    project_ref,
    atlas_ref,
    fp_ref,
    slot_ref,
    base_ref,
    disp_ref,
    out_ref,
    feat,
    chunks,
    cols,
    back,
    mixed,
    pieces,
    picked,
    lib,
    bm,
    tx,
    expand,
    bias,
    wx_all,
    wy_all,
    pz_all,
    wzy,
    acc,
    wide,
    rows_out,
    in_sem,
    a_send,
    a_recv,
    b_send,
    b_recv,
    b_own,
    y_send,
    y_recv,
    g_own,
    g_send,
    g_recv,
):
    s = lax.axis_index("slab")
    p = lax.axis_index("plane")
    px = p // KZ
    pz = lax.rem(p, KZ)
    hid = project_ref.shape[1]
    size = NP * ROWS
    lib = dict(zip(GROUPS, lib))
    sy = s // 2
    core = lax.rem(s, 2)
    chip = lambda d: lax.rem(sy + d + KY, KY) * 2 + core
    above, below, beside = chip(1), chip(-1), s + 1 - 2 * core

    barrier = pltpu.get_barrier_semaphore()

    def greet_plane(i, carry):
        pl.semaphore_signal(
            barrier, inc=1, device_id={"plane": lax.rem(p + i, NP)}, device_id_type=MESH
        )
        return carry

    lax.fori_loop(1, NP, greet_plane, 0)
    for device in (above, below, beside):
        pl.semaphore_signal(barrier, inc=1, device_id={"slab": device}, device_id_type=MESH)

    loads = [
        pltpu.make_async_copy(feat_ref.at[:, z], feat.at[z], in_sem.at[z]) for z in range(ZD)
    ]
    half = px // 2
    cell = 2 * pz + lax.rem(px, 2)
    atlas_load = pltpu.make_async_copy(
        atlas_ref.at[
            :,
            pl.ds(pl.multiple_of(half * 16, 16), 16),
            pl.ds(pl.multiple_of(cell * 128, 128), 128),
        ],
        pieces.at[pl.ds(s * HELD, HELD)],
        in_sem.at[ZD],
    )
    atlas_load.start()
    for load in loads:
        load.start()

    def make_chunks(z):
        loads[z].wait()

        def step(c, carry):
            block = feat[z, c]
            stacked = jnp.concatenate(
                [block[:, q * QW : (q + 1) * QW] for q in range(XQ)], axis=0
            )
            chunks[z, c] = stacked.astype(BF16)
            return carry

        lax.fori_loop(0, NP, step, 0, unroll=4)

    def send_chunks(z):
        def step(i, carry):
            peer = lax.rem(p + i, NP)
            pltpu.make_async_remote_copy(
                chunks.at[z, peer],
                cols.at[z, p],
                a_send.at[z],
                a_recv.at[z],
                device_id={"plane": peer},
                device_id_type=MESH,
            ).start()
            return carry

        lax.fori_loop(1, NP, step, 0)

    for z in range(ZD):
        make_chunks(z)
        cols[z, p] = chunks[z, p]
    def taps_at(index, ref):
        total = jnp.zeros(index.shape, F32)
        for t in range(31):
            total = jnp.where(index == t, ref[p, t], total)
        return total

    def build_rows(m, carry):
        out = lax.broadcasted_iota(jnp.int32, (64, size), 0) + m * 64
        inp = lax.broadcasted_iota(jnp.int32, (64, size), 1)
        row = lambda r: lax.shift_right_logical(r, 4) * 4 + (r & 3)
        quarter = lambda r: lax.shift_right_logical(r, 2) & 3
        weights = taps_at(row(inp) - row(out) + 15, yt_ref)
        for n, shift in enumerate((0, -1, 1)):
            kept = jnp.where(quarter(inp) == quarter(out) + shift, weights, 0.0)
            high, low = split2(kept)
            bm[2 * n, pl.ds(m * 64, 64)] = high
            bm[2 * n + 1, pl.ds(m * 64, 64)] = low
        return carry

    lax.fori_loop(0, size // 64, build_rows, 0)

    def build_x(m, carry):
        k = lax.broadcasted_iota(jnp.int32, (64, QW), 0) + m * 64
        n = lax.broadcasted_iota(jnp.int32, (64, QW), 1)
        high, low = split2(taps_at(k - 128 - n + 15, xt_ref))
        tx[0, pl.ds(m * 64, 64)] = high
        tx[1, pl.ds(m * 64, 64)] = low
        return carry

    lax.fori_loop(0, 8, build_x, 0)

    atlas_load.wait()
    pl.semaphore_wait(barrier, NP - 1 + 3)

    slab_sends = []

    def hand_on(owner, device, index):
        block = pieces.at[pl.ds(owner * HELD, HELD)]
        copy = pltpu.make_async_remote_copy(
            block,
            block,
            y_send.at[len(slab_sends)],
            y_recv.at[index],
            device_id={"slab": device},
            device_id_type=MESH,
        )
        copy.start()
        slab_sends.append(copy)
        return copy

    got = {}
    got["u", 1] = hand_on(s, above, 0)
    got["d", 1] = hand_on(s, below, 4)
    got["c", 0] = hand_on(s, beside, 7)
    for z in range(ZD):
        send_chunks(z)

    expand[...] = jnp.transpose(expand_ref[...].astype(F32)).astype(BF16)
    bias[...] = jnp.transpose(jnp.broadcast_to(bias_ref[...], (hid, hid)))

    def tents_of(n, carry):
        z = n // 8
        y = lax.rem(n, 8) // 2
        xh = lax.rem(n, 2)
        lanes = pl.ds(pl.multiple_of(xh * BLK, BLK), BLK)

        def place(axis, cells):
            base = base_ref[axis, z, xh, y].astype(F32)
            return jnp.clip(disp_ref[axis, z, pl.ds(y, 1), lanes] + base, 0.0, cells - 1.0)

        def tent(axis, cells):
            grid = lax.broadcasted_iota(jnp.int32, (cells, BLK), 0).astype(F32)
            return jnp.maximum(0.0, 1.0 - jnp.abs(place(axis, cells) - grid))

        wy_all[n] = tent(1, TY)
        wx_all[n] = tent(2, TX)
        pz_all[n] = jnp.broadcast_to(place(0, TZ), (8, BLK))
        acc[n] = jnp.zeros((NP, BLK), F32)
        return carry

    tents = lambda: lax.fori_loop(0, NB, tents_of, 0)

    sends = []

    def pass_on(source, target, device, index):
        copy = pltpu.make_async_remote_copy(
            source,
            target,
            g_send.at[len(sends)],
            g_recv.at[index],
            device_id={"plane": device},
            device_id_type=MESH,
        )
        copy.start()
        sends.append(copy)
        return copy

    at = lambda x, z: lax.rem(x + KX, KX) * KZ + lax.rem(z + KZ, KZ)
    column = lambda d: lax.rem(px + d + KX, KX)
    up, down = at(px, pz + 1), at(px, pz - 1)
    right, left = at(px + 1, pz), at(px - 1, pz)
    first, second = pl.ds(0, SLOTS // 2), pl.ds(SLOTS // 2, SLOTS // 2)
    recv = {}

    def spread(dz, source):
        target = lib[dz].at[px]
        recv["r", dz] = pass_on(source, target, right, 7 + dz + 3)
        recv["l", dz] = pass_on(source, target, left, 15 + dz + 3)

    def start_ring():
        for r in range(1, 5):
            got["u", r].wait_recv()
            if r < 4:
                got["u", r + 1] = hand_on(chip(-r), above, r)
            got["c", -r] = hand_on(chip(-r), beside, 7 + r)
            if r < 4:
                got["d", r].wait_recv()
                if r < 3:
                    got["d", r + 1] = hand_on(chip(r), below, 4 + r)
                got["c", r] = hand_on(chip(r), beside, 11 + r)
        for r in range(-4, 4):
            got["c", r].wait_recv()

        def pick(slot, carry):
            tile = jnp.maximum(fp_ref[0, slot], 0)
            picked[slot] = pieces[tile]
            return carry

        lax.fori_loop(0, SLOTS, pick, 0)
        recv["u", 1] = pass_on(picked, lib[-1].at[px], up, 0)
        recv["d", 1] = pass_on(picked, lib[1].at[px], down, 4)
        spread(0, picked)
        copy = pltpu.make_async_copy(picked, lib[0].at[px], g_own)
        copy.start()
        return copy

    def z_step(r):
        recv["u", r].wait_recv()
        dz = -r if r < 4 else 4
        piece = lib[dz].at[px]
        if r < 4:
            recv["u", r + 1] = pass_on(piece, lib[-r - 1 if r < 3 else 4].at[px], up, r)
        spread(dz, piece)
        if r < 4:
            recv["d", r].wait_recv()
            piece = lib[r].at[px]
            if r < 3:
                recv["d", r + 1] = pass_on(piece, lib[r + 1].at[px], down, 4 + r)
            spread(r, piece)

    def x_step(dz):
        recv["r", dz].wait_recv()
        piece = lib[dz].at[column(-1), first]
        recv["rr", dz] = pass_on(piece, piece, right, 23 + dz + 3)
        recv["l", dz].wait_recv()
        piece = lib[dz].at[column(1), second]
        recv["ll", dz] = pass_on(piece, piece, left, 31 + dz + 3)

    def sample(*groups):
        for dz in groups:
            recv["rr", dz].wait_recv()
            recv["ll", dz].wait_recv()
        indices = [lax.rem(pz + dz + KZ, KZ).astype(F32) for dz in groups]

        def step(n, carry):
            slot = slot_ref[n // 8, lax.rem(n, 2), lax.rem(n, 8) // 2]
            wy, wx, place = wy_all[n], wx_all[n], pz_all[n]
            for g, index in enumerate(indices):
                wz = jnp.maximum(0.0, 1.0 - jnp.abs(place - index))
                wzy[g, 0:8] = wz * wy[0:8]
                wzy[g, 8:16] = wz * wy[8:16]
            interp = jnp.concatenate(
                [
                    (wzy[g, j : j + 1] * wx).astype(BF16)
                    for g in range(len(groups))
                    for j in range(TY)
                ],
                axis=0,
            )
            tile = jnp.concatenate(
                [
                    jnp.concatenate(
                        [lib[dz][2 * h + k, slot] for dz in groups for k in range(2)], axis=1
                    )
                    for h in range(2)
                ],
                axis=0,
            )
            acc[n] = acc[n] + dot(tile, interp)
            return carry

        lax.fori_loop(0, NB, step, 0, unroll=4)

    def convolve(z):
        wait_all(cols.at[z, pl.ds(0, NP - 1)], a_recv.at[z])

        def step(m, carry):
            rows = pl.ds(m * 256, 256)
            x = cols[z].reshape(size, QW)
            main = dot(bm[0, rows], x) + dot(bm[1, rows], x)
            before = dot(bm[2, rows], x[:, 128:]) + dot(bm[3, rows], x[:, 128:])
            after = dot(bm[4, rows], x[:, :128]) + dot(bm[5, rows], x[:, :128])
            high, low = split2(jnp.concatenate([before, main, after], axis=1))
            out = dot(high, tx[0]) + dot(low, tx[0]) + dot(high, tx[1])
            back[z, pl.ds(m * 16, 16)] = out.astype(BF16).reshape(16, ROWS, QW)
            return carry

        lax.fori_loop(0, size // 256, step, 0)

        def send(i, carry):
            peer = lax.rem(p + i, NP)
            pltpu.make_async_remote_copy(
                back.at[z, peer],
                mixed.at[z, p],
                b_send.at[z],
                b_recv.at[z],
                device_id={"plane": peer},
                device_id_type=MESH,
            ).start()
            return carry

        lax.fori_loop(1, NP, send, 0)
        own = pltpu.make_async_copy(back.at[z, p], mixed.at[z, p], b_own.at[z])
        own.start()
        return own

    def perceive(z, own):
        wait_all(mixed.at[z, pl.ds(0, NP - 1)], b_recv.at[z])
        own.wait()

        def widen(i, carry):
            two = mixed[z, pl.ds(i * 2, 2)].reshape(2 * ROWS, QW).astype(F32)
            for k in range(2):
                wide[k, pl.ds(pl.multiple_of(i * 32, 32), 32)] = two[:, k * 128 : (k + 1) * 128]
            return carry

        lax.fori_loop(0, NP // 2, widen, 0, unroll=4)

        def step(n, carry):
            y = n // 2
            xh = lax.rem(n, 2)
            x = jnp.concatenate(
                [
                    wide[l, pl.ds(8 * xh + 4 * k + y, NP, stride=ROWS)]
                    for k in range(2)
                    for l in range(2)
                ],
                axis=1,
            ).astype(BF16)
            b = bias[...]
            hidden = dot(expand[...], x) + jnp.concatenate([b] * 4, axis=1)
            acc[z * 8 + n] = acc[z * 8 + n] + dot(project_ref[...], gelu(hidden).astype(BF16))
            return carry

        lax.fori_loop(0, 8, step, 0, unroll=2)

    own_copy = start_ring()
    tents()
    owns = [convolve(0)]
    z_step(1)
    owns.append(convolve(1))
    x_step(0)
    z_step(2)
    owns.append(convolve(2))
    x_step(-1)
    x_step(1)
    z_step(3)
    own_copy.wait()
    sample(0)
    z_step(4)
    x_step(-2)
    x_step(2)
    sample(-1, 1)
    perceive(0, owns[0])
    x_step(-3)
    x_step(3)
    sample(-2, 2)
    perceive(1, owns[1])
    x_step(4)
    perceive(2, owns[2])
    sample(-3, 3)
    sample(4)

    def finish(z, carry):
        def turn(n, carry):
            y = n // 2
            xh = lax.rem(n, 2)
            value = acc[z * 8 + n]
            for k in range(BLK // 128):
                rows_out[xh * 4 + k, pl.ds(y, NP, stride=YR)] = value[:, k * 128 : (k + 1) * 128]
            return carry

        lax.fori_loop(0, 8, turn, 0)

        def write(g, carry):
            rows = pl.ds(pl.multiple_of(g * 8, 8), 8)
            two = jnp.concatenate([rows_out[k, rows] for k in range(8)], axis=1)
            out_ref[pl.ds(g * 2, 2), z] = two.reshape(2, YR, XQ * QW)
            return carry

        lax.fori_loop(0, NP // 2, write, 0)
        return carry

    lax.fori_loop(0, ZD, finish, 0)

    for copy in sends:
        copy.wait_send()
    for copy in slab_sends:
        copy.wait_send()
    for z in range(ZD):
        wait_all(chunks.at[z, pl.ds(0, NP - 1)], a_send.at[z])
        wait_all(back.at[z, pl.ds(0, NP - 1)], b_send.at[z])


def body(
    features,
    x_taps,
    y_taps,
    expand,
    expand_bias,
    project,
    atlas_tiles,
    footprint,
    block_slot,
    tile_base,
    displacement,
):
    size = NP * ROWS
    hid = expand.shape[0]
    hbm = pl.BlockSpec(memory_space=pltpu.HBM)
    scalars = pl.BlockSpec(memory_space=pltpu.SMEM)
    vmem = pl.BlockSpec(memory_space=pltpu.VMEM)
    dma = pltpu.SemaphoreType.DMA
    added = pl.pallas_call(
        block_kernel,
        out_shape=jax.ShapeDtypeStruct(features.shape, F32),
        in_specs=[
            hbm,
            scalars,
            scalars,
            vmem,
            vmem,
            vmem,
            hbm,
            scalars,
            scalars,
            scalars,
            vmem,
        ],
        out_specs=vmem,
        scratch_shapes=[
            pltpu.VMEM((ZD, NP, YR, XQ * QW), F32),
            pltpu.VMEM((ZD, NP, ROWS, QW), BF16),
            pltpu.VMEM((ZD, NP, ROWS, QW), BF16),
            pltpu.VMEM((ZD, NP, ROWS, QW), BF16),
            pltpu.VMEM((ZD, NP, ROWS, QW), BF16),
            pltpu.VMEM((NS * HELD, 16, 128), BF16),
            pltpu.VMEM((SLOTS, 16, 128), BF16),
            [pltpu.VMEM((KX, SLOTS, 16, 128), BF16) for _ in GROUPS],
            pltpu.VMEM((6, size, size), BF16),
            pltpu.VMEM((2, 2 * QW, QW), BF16),
            pltpu.VMEM((hid, NP), BF16),
            pltpu.VMEM((hid, hid), F32),
            pltpu.VMEM((NB, TX, BLK), F32),
            pltpu.VMEM((NB, TY, BLK), F32),
            pltpu.VMEM((NB, 8, BLK), F32),
            pltpu.VMEM((2, TY, BLK), F32),
            pltpu.VMEM((NB, NP, BLK), F32),
            pltpu.VMEM((2, size, 128), F32),
            pltpu.VMEM((8, NP * YR, 128), F32),
            dma((ZD + 1,)),
            dma((ZD,)),
            dma((ZD,)),
            dma((ZD,)),
            dma((ZD,)),
            dma((ZD,)),
            dma((15,)),
            dma((15,)),
            dma(()),
            dma((39,)),
            dma((39,)),
        ],
        compiler_params=pltpu.CompilerParams(
            collective_id=0, has_side_effects=True, vmem_limit_bytes=60 * 1024 * 1024
        ),
        cost_estimate=pl.CostEstimate(
            flops=10_000_000_000, bytes_accessed=10_000_000, transcendentals=1_600_000
        ),
    )(
        features,
        x_taps,
        y_taps,
        expand.T,
        expand_bias.reshape(1, hid),
        project,
        atlas_tiles,
        footprint,
        jnp.swapaxes(block_slot, 1, 2),
        jnp.swapaxes(tile_base, 2, 3),
        displacement,
    )
    return features + added


def solution(mesh):
    return jax.shard_map(
        body,
        mesh=mesh,
        in_specs=(
            P(None, "slab", "plane", None),
            P(),
            P(),
            P(),
            P(),
            P(),
            P("slab", None, None),
            P("slab", None),
            P("slab", "plane", None),
            P(None, "slab", "plane", None),
            P(None, "slab", "plane", None),
        ),
        out_specs=P(None, "slab", "plane", None),
        check_vma=False,
    )
```

```python
import functools

import jax
import jax.numpy as jnp
from jax import lax
from jax.experimental import pallas as pl
from jax.experimental.pallas import tpu as pltpu
from jax.sharding import PartitionSpec as P

TZ = 8
TY = 16
TX = 16
BLK = 512
KZ = 8
KX = 4
NP = KX * KZ
NS = 16
KY = NS // 2
CAP = 2
SLOTS = NS * CAP
HELD = 8
ZD = 3
YR = 4
XQ = 4
QW = 256
ROWS = XQ * YR
NB = ZD * YR * 2
RU, RD = 2, 2
GROUPS = tuple(range(-RU, RD + 1))
DIRECT = tuple(range(RD + 1, KZ - RU))
F32 = jnp.float32
BF16 = jnp.bfloat16
MESH = pl.DeviceIdType.MESH


def dot(a, b):
    return jnp.dot(a, b, preferred_element_type=F32)


def split2(value):
    high = value.astype(BF16)
    return high, (value - high.astype(F32)).astype(BF16)


def gelu(a):
    inner = a * (0.7978845608028654 + (0.7978845608028654 * 0.044715) * (a * a))
    half = 0.5 * a
    return half + half * jnp.tanh(inner)


def wait_all(ref, sem):
    pltpu.make_async_copy(ref, ref, sem).wait()


def block_kernel(
    feat_ref,
    xt_ref,
    yt_ref,
    expand_ref,
    bias_ref,
    project_ref,
    atlas_ref,
    fp_ref,
    row_ref,
    slot_ref,
    base_ref,
    disp_ref,
    out_ref,
    feat,
    chunks,
    cols,
    back,
    mixed,
    pieces,
    picked,
    lib,
    straight,
    held,
    stage,
    rows_all,
    wanted,
    bm,
    tx,
    expand,
    bias,
    wx_all,
    wy_all,
    pz_all,
    wzy,
    acc,
    wide,
    rows_out,
    in_sem,
    a_send,
    a_recv,
    b_send,
    b_recv,
    b_own,
    y_send,
    y_recv,
    g_own,
    g_send,
    g_recv,
    f_send,
    f_recv,
    f_local,
    d_load,
    d_send,
    d_recv,
):
    s = lax.axis_index("slab")
    p = lax.axis_index("plane")
    px = p // KZ
    pz = lax.rem(p, KZ)
    hid = project_ref.shape[1]
    size = NP * ROWS
    lib = dict(zip(GROUPS, lib))
    straight, held, stage = (dict(zip(DIRECT, refs)) for refs in (straight, held, stage))
    sy = s // 2
    core = lax.rem(s, 2)
    chip = lambda d: lax.rem(sy + d + KY, KY) * 2 + core
    beside = s + 1 - 2 * core
    mine = pl.ds((core * KY + sy) * HELD, HELD)
    near = pl.ds(core * KY * HELD, KY * HELD)
    far = pl.ds((1 - core) * KY * HELD, KY * HELD)

    barrier = pltpu.get_barrier_semaphore()

    def greet_plane(i, carry):
        pl.semaphore_signal(
            barrier, inc=1, device_id={"plane": lax.rem(p + i, NP)}, device_id_type=MESH
        )
        return carry

    lax.fori_loop(1, NP, greet_plane, 0)

    def greet_slab(i, carry):
        pl.semaphore_signal(
            barrier, inc=1, device_id={"slab": lax.rem(s + i, NS)}, device_id_type=MESH
        )
        return carry

    lax.fori_loop(1, NS, greet_slab, 0)

    loads = [
        pltpu.make_async_copy(feat_ref.at[:, z], feat.at[z], in_sem.at[z]) for z in range(ZD)
    ]
    half = px // 2
    cell = 2 * pz + lax.rem(px, 2)
    atlas_load = pltpu.make_async_copy(
        atlas_ref.at[
            :,
            pl.ds(pl.multiple_of(half * 16, 16), 16),
            pl.ds(pl.multiple_of(cell * 128, 128), 128),
        ],
        pieces.at[mine],
        in_sem.at[ZD],
    )
    atlas_load.start()
    held_loads = []
    for n, dz in enumerate(DIRECT):
        for q in range(KX):
            start = (2 * lax.rem(pz + dz + KZ, KZ) + q % 2) * 128
            held_loads.append(
                pltpu.make_async_copy(
                    atlas_ref.at[
                        :, pl.ds(q // 2 * 16, 16), pl.ds(pl.multiple_of(start, 128), 128)
                    ],
                    held[dz].at[q],
                    d_load.at[n * KX + q],
                )
            )
    for load in loads + held_loads:
        load.start()

    def make_chunks(z):
        loads[z].wait()

        def step(c, carry):
            block = feat[z, c]
            stacked = jnp.concatenate(
                [block[:, q * QW : (q + 1) * QW] for q in range(XQ)], axis=0
            )
            chunks[z, c] = stacked.astype(BF16)
            return carry

        lax.fori_loop(0, NP, step, 0, unroll=4)

    def send_chunks(z):
        def step(i, carry):
            peer = lax.rem(p + i, NP)
            pltpu.make_async_remote_copy(
                chunks.at[z, peer],
                cols.at[z, p],
                a_send.at[z],
                a_recv.at[z],
                device_id={"plane": peer},
                device_id_type=MESH,
            ).start()
            return carry

        lax.fori_loop(1, NP, step, 0)

    for z in range(ZD):
        make_chunks(z)
        cols[z, p] = chunks[z, p]
    def taps_at(index, ref):
        total = jnp.zeros(index.shape, F32)
        for t in range(31):
            total = jnp.where(index == t, ref[p, t], total)
        return total

    def build_rows(m, carry):
        out = lax.broadcasted_iota(jnp.int32, (64, size), 0) + m * 64
        inp = lax.broadcasted_iota(jnp.int32, (64, size), 1)
        row = lambda r: lax.shift_right_logical(r, 4) * 4 + (r & 3)
        quarter = lambda r: lax.shift_right_logical(r, 2) & 3
        weights = taps_at(row(inp) - row(out) + 15, yt_ref)
        for n, shift in enumerate((0, -1, 1)):
            kept = jnp.where(quarter(inp) == quarter(out) + shift, weights, 0.0)
            high, low = split2(kept)
            bm[2 * n, pl.ds(m * 64, 64)] = high
            bm[2 * n + 1, pl.ds(m * 64, 64)] = low
        return carry

    lax.fori_loop(0, size // 64, build_rows, 0)

    def build_x(m, carry):
        k = lax.broadcasted_iota(jnp.int32, (64, QW), 0) + m * 64
        n = lax.broadcasted_iota(jnp.int32, (64, QW), 1)
        high, low = split2(taps_at(k - 128 - n + 15, xt_ref))
        tx[0, pl.ds(m * 64, 64)] = high
        tx[1, pl.ds(m * 64, 64)] = low
        return carry

    lax.fori_loop(0, 8, build_x, 0)

    expand[...] = jnp.transpose(expand_ref[...].astype(F32)).astype(BF16)
    bias[...] = jnp.transpose(jnp.broadcast_to(bias_ref[...], (hid, hid)))

    def tents_of(n, carry):
        z = n // 8
        y = lax.rem(n, 8) // 2
        xh = lax.rem(n, 2)
        lanes = pl.ds(pl.multiple_of(xh * BLK, BLK), BLK)

        def place(axis, cells):
            base = base_ref[axis, z, xh, y].astype(F32)
            return jnp.clip(disp_ref[axis, z, pl.ds(y, 1), lanes] + base, 0.0, cells - 1.0)

        def tent(axis, cells):
            grid = lax.broadcasted_iota(jnp.int32, (cells, BLK), 0).astype(F32)
            return jnp.maximum(0.0, 1.0 - jnp.abs(place(axis, cells) - grid))

        wy_all[n] = tent(1, TY)
        wx_all[n] = tent(2, TX)
        pz_all[n] = jnp.broadcast_to(place(0, TZ), (8, BLK))
        acc[n] = jnp.zeros((NP, BLK), F32)
        return carry

    lax.fori_loop(0, NB, tents_of, 0)

    atlas_load.wait()
    pl.semaphore_wait(barrier, NP - 1 + NS - 1)

    def send_row(i, carry):
        pltpu.make_async_remote_copy(
            row_ref,
            rows_all.at[s],
            f_send,
            f_recv,
            device_id={"slab": lax.rem(s + i, NS)},
            device_id_type=MESH,
        ).start()
        return carry

    lax.fori_loop(1, NS, send_row, 0)
    rows_all[s] = row_ref[...]

    def send_piece(i, carry):
        pltpu.make_async_remote_copy(
            pieces.at[mine],
            pieces.at[mine],
            y_send.at[0],
            y_recv.at[0],
            device_id={"slab": chip(i)},
            device_id_type=MESH,
        ).start()
        return carry

    lax.fori_loop(1, KY, send_piece, 0)
    for z in range(ZD):
        send_chunks(z)

    sends = []

    def pass_on(source, target, device, index):
        copy = pltpu.make_async_remote_copy(
            source,
            target,
            g_send.at[len(sends)],
            g_recv.at[index],
            device_id={"plane": device},
            device_id_type=MESH,
        )
        copy.start()
        sends.append(copy)
        return copy

    at = lambda x, z: lax.rem(x + KX, KX) * KZ + lax.rem(z + KZ, KZ)
    recv = {}
    around = (("r", 1), ("l", -1), ("o", 2))

    def spread(dz, source):
        for n, (way, dx) in enumerate(around):
            recv[way, dz] = pass_on(source, lib[dz].at[px], at(px + dx, pz), 7 + 8 * n + dz + 3)

    def start_ring():
        wait_all(pieces.at[pl.ds(0, (KY - 1) * HELD)], y_recv.at[0])
        pltpu.make_async_remote_copy(
            pieces.at[near],
            pieces.at[near],
            y_send.at[1],
            y_recv.at[1],
            device_id={"slab": beside},
            device_id_type=MESH,
        ).start()
        wait_all(pieces.at[far], y_recv.at[1])

        def pick(slot, carry):
            tile = jnp.maximum(fp_ref[0, slot], 0)
            owner = tile // HELD
            place = lax.rem(owner, 2) * KY + owner // 2
            picked[slot] = pieces[place * HELD + lax.rem(tile, HELD)]
            return carry

        lax.fori_loop(0, SLOTS, pick, 0)
        spread(0, picked)
        for dz in GROUPS:
            if dz:
                recv["z", dz] = pass_on(picked, lib[dz].at[px], at(px, pz - dz), dz + 3)
        copy = pltpu.make_async_copy(picked, lib[0].at[px], g_own)
        copy.start()
        return copy

    def start_direct():
        wait_all(rows_all.at[pl.ds(0, NS - 1)], f_recv)
        local = pltpu.make_async_copy(rows_all, wanted, f_local)
        local.start()
        for load in held_loads:
            load.wait()
        local.wait()
        for n, dz in enumerate(DIRECT):

            def fill(j, carry):
                tile = wanted[j // CAP, 0, s * CAP + lax.rem(j, CAP)] - s * HELD
                tile = jnp.clip(tile, 0, HELD - 1)
                for q in range(KX):
                    stage[dz][j, q] = held[dz][q, tile]
                return carry

            lax.fori_loop(0, SLOTS, fill, 0, unroll=2)

            def send(i, carry):
                peer = lax.rem(s + i, NS)
                pltpu.make_async_remote_copy(
                    stage[dz].at[pl.ds(peer * CAP, CAP)],
                    straight[dz].at[pl.ds(s * CAP, CAP)],
                    d_send.at[n],
                    d_recv.at[n],
                    device_id={"slab": peer},
                    device_id_type=MESH,
                ).start()
                return carry

            lax.fori_loop(1, NS, send, 0)
            straight[dz][pl.ds(s * CAP, CAP)] = stage[dz][pl.ds(s * CAP, CAP)]

    def z_step(dz):
        recv["z", dz].wait_recv()
        spread(dz, lib[dz].at[px])

    def sample(*groups):
        for dz in groups:
            if dz in GROUPS:
                for way, _ in around:
                    recv[way, dz].wait_recv()
            else:
                wait_all(straight[dz].at[pl.ds(0, SLOTS - CAP)], d_recv.at[DIRECT.index(dz)])

        def part(dz, q, slot):
            return lib[dz][q, slot] if dz in GROUPS else straight[dz][slot, q]

        indices = [lax.rem(pz + dz + KZ, KZ).astype(F32) for dz in groups]

        def step(n, carry):
            slot = slot_ref[n // 8, lax.rem(n, 2), lax.rem(n, 8) // 2]
            wy, wx, place = wy_all[n], wx_all[n], pz_all[n]
            for g, index in enumerate(indices):
                wz = jnp.maximum(0.0, 1.0 - jnp.abs(place - index))
                wzy[g, 0:8] = wz * wy[0:8]
                wzy[g, 8:16] = wz * wy[8:16]
            interp = jnp.concatenate(
                [
                    (wzy[g, j : j + 1] * wx).astype(BF16)
                    for g in range(len(groups))
                    for j in range(TY)
                ],
                axis=0,
            )
            tile = jnp.concatenate(
                [
                    jnp.concatenate(
                        [part(dz, 2 * h + k, slot) for dz in groups for k in range(2)], axis=1
                    )
                    for h in range(2)
                ],
                axis=0,
            )
            acc[n] = acc[n] + dot(tile, interp)
            return carry

        lax.fori_loop(0, NB, step, 0, unroll=4)

    def convolve(z):
        wait_all(cols.at[z, pl.ds(0, NP - 1)], a_recv.at[z])

        def step(m, carry):
            rows = pl.ds(m * 256, 256)
            x = cols[z].reshape(size, QW)
            main = dot(bm[0, rows], x) + dot(bm[1, rows], x)
            before = dot(bm[2, rows], x[:, 128:]) + dot(bm[3, rows], x[:, 128:])
            after = dot(bm[4, rows], x[:, :128]) + dot(bm[5, rows], x[:, :128])
            high, low = split2(jnp.concatenate([before, main, after], axis=1))
            out = dot(high, tx[0]) + dot(low, tx[0]) + dot(high, tx[1])
            back[z, pl.ds(m * 16, 16)] = out.astype(BF16).reshape(16, ROWS, QW)
            return carry

        lax.fori_loop(0, size // 256, step, 0)

        def send(i, carry):
            peer = lax.rem(p + i, NP)
            pltpu.make_async_remote_copy(
                back.at[z, peer],
                mixed.at[z, p],
                b_send.at[z],
                b_recv.at[z],
                device_id={"plane": peer},
                device_id_type=MESH,
            ).start()
            return carry

        lax.fori_loop(1, NP, send, 0)
        own = pltpu.make_async_copy(back.at[z, p], mixed.at[z, p], b_own.at[z])
        own.start()
        return own

    def perceive(z, own):
        wait_all(mixed.at[z, pl.ds(0, NP - 1)], b_recv.at[z])
        own.wait()

        def widen(i, carry):
            two = mixed[z, pl.ds(i * 2, 2)].reshape(2 * ROWS, QW).astype(F32)
            for k in range(2):
                wide[k, pl.ds(pl.multiple_of(i * 32, 32), 32)] = two[:, k * 128 : (k + 1) * 128]
            return carry

        lax.fori_loop(0, NP // 2, widen, 0, unroll=4)

        def step(n, carry):
            y = n // 2
            xh = lax.rem(n, 2)
            x = jnp.concatenate(
                [
                    wide[l, pl.ds(8 * xh + 4 * k + y, NP, stride=ROWS)]
                    for k in range(2)
                    for l in range(2)
                ],
                axis=1,
            ).astype(BF16)
            b = bias[...]
            hidden = dot(expand[...], x) + jnp.concatenate([b] * 4, axis=1)
            acc[z * 8 + n] = acc[z * 8 + n] + dot(project_ref[...], gelu(hidden).astype(BF16))
            return carry

        lax.fori_loop(0, 8, step, 0, unroll=2)

    start_direct()
    own_copy = start_ring()
    owns = [convolve(0)]
    z_step(1)
    z_step(-1)
    z_step(2)
    z_step(-2)
    owns.append(convolve(1))
    owns.append(convolve(2))
    own_copy.wait()
    sample(0)
    sample(3)
    perceive(0, owns[0])
    sample(-1, 1)
    perceive(1, owns[1])
    sample(4)
    sample(-2, 2)
    perceive(2, owns[2])
    sample(5)

    def finish(z, carry):
        def turn(n, carry):
            y = n // 2
            xh = lax.rem(n, 2)
            value = acc[z * 8 + n]
            for k in range(BLK // 128):
                rows_out[xh * 4 + k, pl.ds(y, NP, stride=YR)] = value[:, k * 128 : (k + 1) * 128]
            return carry

        lax.fori_loop(0, 8, turn, 0)

        def write(g, carry):
            rows = pl.ds(pl.multiple_of(g * 8, 8), 8)
            two = jnp.concatenate([rows_out[k, rows] for k in range(8)], axis=1)
            out_ref[pl.ds(g * 2, 2), z] = two.reshape(2, YR, XQ * QW)
            return carry

        lax.fori_loop(0, NP // 2, write, 0)
        return carry

    lax.fori_loop(0, ZD, finish, 0)

    for copy in sends:
        copy.wait_send()
    wait_all(pieces.at[pl.ds(0, (KY - 1) * HELD)], y_send.at[0])
    wait_all(pieces.at[near], y_send.at[1])
    wait_all(rows_all.at[pl.ds(0, NS - 1)], f_send)
    for n, dz in enumerate(DIRECT):
        wait_all(stage[dz].at[pl.ds(0, SLOTS - CAP)], d_send.at[n])
    for z in range(ZD):
        wait_all(chunks.at[z, pl.ds(0, NP - 1)], a_send.at[z])
        wait_all(back.at[z, pl.ds(0, NP - 1)], b_send.at[z])


def body(
    features,
    x_taps,
    y_taps,
    expand,
    expand_bias,
    project,
    atlas_tiles,
    footprint,
    block_slot,
    tile_base,
    displacement,
):
    size = NP * ROWS
    hid = expand.shape[0]
    hbm = pl.BlockSpec(memory_space=pltpu.HBM)
    scalars = pl.BlockSpec(memory_space=pltpu.SMEM)
    vmem = pl.BlockSpec(memory_space=pltpu.VMEM)
    dma = pltpu.SemaphoreType.DMA
    added = pl.pallas_call(
        block_kernel,
        out_shape=jax.ShapeDtypeStruct(features.shape, F32),
        in_specs=[
            hbm,
            scalars,
            scalars,
            vmem,
            vmem,
            vmem,
            hbm,
            scalars,
            vmem,
            scalars,
            scalars,
            vmem,
        ],
        out_specs=vmem,
        scratch_shapes=[
            pltpu.VMEM((ZD, NP, YR, XQ * QW), F32),
            pltpu.VMEM((ZD, NP, ROWS, QW), BF16),
            pltpu.VMEM((ZD, NP, ROWS, QW), BF16),
            pltpu.VMEM((ZD, NP, ROWS, QW), BF16),
            pltpu.VMEM((ZD, NP, ROWS, QW), BF16),
            pltpu.VMEM((NS * HELD, 16, 128), BF16),
            pltpu.VMEM((SLOTS, 16, 128), BF16),
            [pltpu.VMEM((KX, SLOTS, 16, 128), BF16) for _ in GROUPS],
            [pltpu.VMEM((SLOTS, KX, 16, 128), BF16) for _ in DIRECT],
            [pltpu.VMEM((KX, HELD, 16, 128), BF16) for _ in DIRECT],
            [pltpu.VMEM((SLOTS, KX, 16, 128), BF16) for _ in DIRECT],
            pltpu.VMEM((NS, 1, SLOTS), jnp.int32),
            pltpu.SMEM((NS, 1, SLOTS), jnp.int32),
            pltpu.VMEM((6, size, size), BF16),
            pltpu.VMEM((2, 2 * QW, QW), BF16),
            pltpu.VMEM((hid, NP), BF16),
            pltpu.VMEM((hid, hid), F32),
            pltpu.VMEM((NB, TX, BLK), F32),
            pltpu.VMEM((NB, TY, BLK), F32),
            pltpu.VMEM((NB, 8, BLK), F32),
            pltpu.VMEM((2, TY, BLK), F32),
            pltpu.VMEM((NB, NP, BLK), F32),
            pltpu.VMEM((2, size, 128), F32),
            pltpu.VMEM((8, NP * YR, 128), F32),
            dma((ZD + 1,)),
            dma((ZD,)),
            dma((ZD,)),
            dma((ZD,)),
            dma((ZD,)),
            dma((ZD,)),
            dma((2,)),
            dma((2,)),
            dma(()),
            dma((39,)),
            dma((39,)),
            dma(()),
            dma(()),
            dma(()),
            dma((len(DIRECT) * KX,)),
            dma((len(DIRECT),)),
            dma((len(DIRECT),)),
        ],
        compiler_params=pltpu.CompilerParams(
            collective_id=0, has_side_effects=True, vmem_limit_bytes=60 * 1024 * 1024
        ),
        cost_estimate=pl.CostEstimate(
            flops=10_000_000_000, bytes_accessed=10_000_000, transcendentals=1_600_000
        ),
    )(
        features,
        x_taps,
        y_taps,
        expand.T,
        expand_bias.reshape(1, hid),
        project,
        atlas_tiles,
        footprint,
        footprint,
        jnp.swapaxes(block_slot, 1, 2),
        jnp.swapaxes(tile_base, 2, 3),
        displacement,
    )
    return features + added


def solution(mesh):
    return jax.shard_map(
        body,
        mesh=mesh,
        in_specs=(
            P(None, "slab", "plane", None),
            P(),
            P(),
            P(),
            P(),
            P(),
            P("slab", None, None),
            P("slab", None),
            P("slab", "plane", None),
            P(None, "slab", "plane", None),
            P(None, "slab", "plane", None),
        ),
        out_specs=P(None, "slab", "plane", None),
        check_vma=False,
    )
```

```python
import functools

import jax
import jax.numpy as jnp
from jax import lax
from jax.experimental import pallas as pl
from jax.experimental.pallas import tpu as pltpu
from jax.sharding import PartitionSpec as P

TZ = 8
TY = 16
TX = 16
BLK = 512
KZ = 8
KX = 4
NP = KX * KZ
NS = 16
KY = NS // 2
CAP = 2
SLOTS = NS * CAP
HELD = 8
ZD = 3
YR = 4
XQ = 4
QW = 256
ROWS = XQ * YR
NB = ZD * YR * 2
RU, RD = 1, 2
GROUPS = tuple(range(-RU, RD + 1))
DIRECT = tuple(range(RD + 1, KZ - RU))
F32 = jnp.float32
BF16 = jnp.bfloat16
MESH = pl.DeviceIdType.MESH


def dot(a, b):
    return jnp.dot(a, b, preferred_element_type=F32)


def split2(value):
    high = value.astype(BF16)
    return high, (value - high.astype(F32)).astype(BF16)


def gelu(a):
    inner = a * (0.7978845608028654 + (0.7978845608028654 * 0.044715) * (a * a))
    half = 0.5 * a
    return half + half * jnp.tanh(inner)


def wait_all(ref, sem):
    pltpu.make_async_copy(ref, ref, sem).wait()


def block_kernel(
    feat_ref,
    xt_ref,
    yt_ref,
    expand_ref,
    bias_ref,
    project_ref,
    atlas_ref,
    fp_ref,
    row_ref,
    slot_ref,
    base_ref,
    disp_ref,
    out_ref,
    feat,
    chunks,
    cols,
    back,
    mixed,
    pieces,
    picked,
    lib,
    straight,
    held,
    stage,
    rows_all,
    wanted,
    bm,
    tx,
    expand,
    bias,
    wx_all,
    wy_all,
    pz_all,
    wzy,
    acc,
    wide,
    rows_out,
    in_sem,
    a_send,
    a_recv,
    b_send,
    b_recv,
    b_own,
    y_send,
    y_recv,
    g_own,
    g_send,
    g_recv,
    f_send,
    f_recv,
    f_local,
    d_load,
    d_send,
    d_recv,
):
    s = lax.axis_index("slab")
    p = lax.axis_index("plane")
    px = p // KZ
    pz = lax.rem(p, KZ)
    hid = project_ref.shape[1]
    size = NP * ROWS
    lib = dict(zip(GROUPS, lib))
    straight, held, stage = (dict(zip(DIRECT, refs)) for refs in (straight, held, stage))
    sy = s // 2
    core = lax.rem(s, 2)
    chip = lambda d: lax.rem(sy + d + KY, KY) * 2 + core
    beside = s + 1 - 2 * core
    mine = pl.ds((core * KY + sy) * HELD, HELD)
    near = pl.ds(core * KY * HELD, KY * HELD)
    far = pl.ds((1 - core) * KY * HELD, KY * HELD)

    barrier = pltpu.get_barrier_semaphore()

    def greet_plane(i, carry):
        pl.semaphore_signal(
            barrier, inc=1, device_id={"plane": lax.rem(p + i, NP)}, device_id_type=MESH
        )
        return carry

    lax.fori_loop(1, NP, greet_plane, 0)

    def greet_slab(i, carry):
        pl.semaphore_signal(
            barrier, inc=1, device_id={"slab": lax.rem(s + i, NS)}, device_id_type=MESH
        )
        return carry

    lax.fori_loop(1, NS, greet_slab, 0)

    loads = [
        pltpu.make_async_copy(feat_ref.at[:, z], feat.at[z], in_sem.at[z]) for z in range(ZD)
    ]
    half = px // 2
    cell = 2 * pz + lax.rem(px, 2)
    atlas_load = pltpu.make_async_copy(
        atlas_ref.at[
            :,
            pl.ds(pl.multiple_of(half * 16, 16), 16),
            pl.ds(pl.multiple_of(cell * 128, 128), 128),
        ],
        pieces.at[mine],
        in_sem.at[ZD],
    )
    atlas_load.start()
    held_loads = []
    for n, dz in enumerate(DIRECT):
        for q in range(KX):
            start = (2 * lax.rem(pz + dz + KZ, KZ) + q % 2) * 128
            held_loads.append(
                pltpu.make_async_copy(
                    atlas_ref.at[
                        :, pl.ds(q // 2 * 16, 16), pl.ds(pl.multiple_of(start, 128), 128)
                    ],
                    held[dz].at[q],
                    d_load.at[n * KX + q],
                )
            )
    for load in loads + held_loads:
        load.start()

    def make_chunks(z):
        loads[z].wait()

        def step(c, carry):
            block = feat[z, c]
            stacked = jnp.concatenate(
                [block[:, q * QW : (q + 1) * QW] for q in range(XQ)], axis=0
            )
            chunks[z, c] = stacked.astype(BF16)
            return carry

        lax.fori_loop(0, NP, step, 0, unroll=4)

    def send_chunks(z):
        def step(i, carry):
            peer = lax.rem(p + i, NP)
            pltpu.make_async_remote_copy(
                chunks.at[z, peer],
                cols.at[z, p],
                a_send.at[z],
                a_recv.at[z],
                device_id={"plane": peer},
                device_id_type=MESH,
            ).start()
            return carry

        lax.fori_loop(1, NP, step, 0)

    for z in range(ZD):
        make_chunks(z)
        cols[z, p] = chunks[z, p]
    def taps_at(index, ref):
        total = jnp.zeros(index.shape, F32)
        for t in range(31):
            total = jnp.where(index == t, ref[p, t], total)
        return total

    def build_rows(m, carry):
        out = lax.broadcasted_iota(jnp.int32, (64, size), 0) + m * 64
        inp = lax.broadcasted_iota(jnp.int32, (64, size), 1)
        row = lambda r: lax.shift_right_logical(r, 4) * 4 + (r & 3)
        quarter = lambda r: lax.shift_right_logical(r, 2) & 3
        weights = taps_at(row(inp) - row(out) + 15, yt_ref)
        for n, shift in enumerate((0, -1, 1)):
            kept = jnp.where(quarter(inp) == quarter(out) + shift, weights, 0.0)
            high, low = split2(kept)
            bm[2 * n, pl.ds(m * 64, 64)] = high
            bm[2 * n + 1, pl.ds(m * 64, 64)] = low
        return carry

    lax.fori_loop(0, size // 64, build_rows, 0)

    def build_x(m, carry):
        k = lax.broadcasted_iota(jnp.int32, (64, QW), 0) + m * 64
        n = lax.broadcasted_iota(jnp.int32, (64, QW), 1)
        high, low = split2(taps_at(k - 128 - n + 15, xt_ref))
        tx[0, pl.ds(m * 64, 64)] = high
        tx[1, pl.ds(m * 64, 64)] = low
        return carry

    lax.fori_loop(0, 8, build_x, 0)

    expand[...] = jnp.transpose(expand_ref[...].astype(F32)).astype(BF16)
    bias[...] = jnp.transpose(jnp.broadcast_to(bias_ref[...], (hid, hid)))

    def tents_of(n, carry):
        z = n // 8
        y = lax.rem(n, 8) // 2
        xh = lax.rem(n, 2)
        lanes = pl.ds(pl.multiple_of(xh * BLK, BLK), BLK)

        def place(axis, cells):
            base = base_ref[axis, z, xh, y].astype(F32)
            return jnp.clip(disp_ref[axis, z, pl.ds(y, 1), lanes] + base, 0.0, cells - 1.0)

        def tent(axis, cells):
            grid = lax.broadcasted_iota(jnp.int32, (cells, BLK), 0).astype(F32)
            return jnp.maximum(0.0, 1.0 - jnp.abs(place(axis, cells) - grid))

        wy_all[n] = tent(1, TY)
        wx_all[n] = tent(2, TX)
        pz_all[n] = jnp.broadcast_to(place(0, TZ), (8, BLK))
        acc[n] = jnp.zeros((NP, BLK), F32)
        return carry

    lax.fori_loop(0, NB, tents_of, 0)

    atlas_load.wait()
    pl.semaphore_wait(barrier, NP - 1 + NS - 1)

    def send_row(i, carry):
        pltpu.make_async_remote_copy(
            row_ref,
            rows_all.at[s],
            f_send,
            f_recv,
            device_id={"slab": lax.rem(s + i, NS)},
            device_id_type=MESH,
        ).start()
        return carry

    lax.fori_loop(1, NS, send_row, 0)
    rows_all[s] = row_ref[...]

    def send_piece(i, carry):
        pltpu.make_async_remote_copy(
            pieces.at[mine],
            pieces.at[mine],
            y_send.at[0],
            y_recv.at[0],
            device_id={"slab": chip(i)},
            device_id_type=MESH,
        ).start()
        return carry

    lax.fori_loop(1, KY, send_piece, 0)
    for z in range(ZD):
        send_chunks(z)

    sends = []

    def pass_on(source, target, device, index):
        copy = pltpu.make_async_remote_copy(
            source,
            target,
            g_send.at[len(sends)],
            g_recv.at[index],
            device_id={"plane": device},
            device_id_type=MESH,
        )
        copy.start()
        sends.append(copy)
        return copy

    at = lambda x, z: lax.rem(x + KX, KX) * KZ + lax.rem(z + KZ, KZ)
    recv = {}
    around = (("r", 1), ("l", -1), ("o", 2))

    def spread(dz, source):
        for n, (way, dx) in enumerate(around):
            recv[way, dz] = pass_on(source, lib[dz].at[px], at(px + dx, pz), 7 + 8 * n + dz + 3)

    def hand_over():
        wait_all(pieces.at[pl.ds(0, (KY - 1) * HELD)], y_recv.at[0])
        pltpu.make_async_remote_copy(
            pieces.at[near],
            pieces.at[near],
            y_send.at[1],
            y_recv.at[1],
            device_id={"slab": beside},
            device_id_type=MESH,
        ).start()

    def start_ring():
        wait_all(pieces.at[far], y_recv.at[1])

        def pick(slot, carry):
            tile = jnp.maximum(fp_ref[0, slot], 0)
            owner = tile // HELD
            place = lax.rem(owner, 2) * KY + owner // 2
            picked[slot] = pieces[place * HELD + lax.rem(tile, HELD)]
            return carry

        lax.fori_loop(0, SLOTS, pick, 0)
        spread(0, picked)
        for dz in GROUPS:
            if dz:
                recv["z", dz] = pass_on(picked, lib[dz].at[px], at(px, pz - dz), dz + 3)
        copy = pltpu.make_async_copy(picked, lib[0].at[px], g_own)
        copy.start()
        return copy

    def start_direct():
        wait_all(rows_all.at[pl.ds(0, NS - 1)], f_recv)
        local = pltpu.make_async_copy(rows_all, wanted, f_local)
        local.start()
        for load in held_loads:
            load.wait()
        local.wait()
        for n, dz in enumerate(DIRECT):

            def fill(j, carry):
                tile = wanted[j // CAP, 0, s * CAP + lax.rem(j, CAP)] - s * HELD
                tile = jnp.clip(tile, 0, HELD - 1)
                for q in range(KX):
                    stage[dz][j, q] = held[dz][q, tile]
                return carry

            lax.fori_loop(0, SLOTS, fill, 0, unroll=2)

            def send(i, carry):
                peer = lax.rem(s + i, NS)
                pltpu.make_async_remote_copy(
                    stage[dz].at[pl.ds(peer * CAP, CAP)],
                    straight[dz].at[pl.ds(s * CAP, CAP)],
                    d_send.at[n],
                    d_recv.at[n],
                    device_id={"slab": peer},
                    device_id_type=MESH,
                ).start()
                return carry

            lax.fori_loop(1, NS, send, 0)
            straight[dz][pl.ds(s * CAP, CAP)] = stage[dz][pl.ds(s * CAP, CAP)]

    def z_step(dz):
        recv["z", dz].wait_recv()
        spread(dz, lib[dz].at[px])

    def sample(*groups):
        for dz in groups:
            if dz in GROUPS:
                for way, _ in around:
                    recv[way, dz].wait_recv()
            else:
                wait_all(straight[dz].at[pl.ds(0, SLOTS - CAP)], d_recv.at[DIRECT.index(dz)])

        def part(dz, q, slot):
            return lib[dz][q, slot] if dz in GROUPS else straight[dz][slot, q]

        indices = [lax.rem(pz + dz + KZ, KZ).astype(F32) for dz in groups]

        def step(n, carry):
            slot = slot_ref[n // 8, lax.rem(n, 2), lax.rem(n, 8) // 2]
            wy, wx, place = wy_all[n], wx_all[n], pz_all[n]
            for g, index in enumerate(indices):
                wz = jnp.maximum(0.0, 1.0 - jnp.abs(place - index))
                wzy[g, 0:8] = wz * wy[0:8]
                wzy[g, 8:16] = wz * wy[8:16]
            interp = jnp.concatenate(
                [
                    (wzy[g, j : j + 1] * wx).astype(BF16)
                    for g in range(len(groups))
                    for j in range(TY)
                ],
                axis=0,
            )
            tile = jnp.concatenate(
                [
                    jnp.concatenate(
                        [part(dz, 2 * h + k, slot) for dz in groups for k in range(2)], axis=1
                    )
                    for h in range(2)
                ],
                axis=0,
            )
            acc[n] = acc[n] + dot(tile, interp)
            return carry

        lax.fori_loop(0, NB, step, 0, unroll=4)

    def convolve(z):
        wait_all(cols.at[z, pl.ds(0, NP - 1)], a_recv.at[z])

        def step(m, carry):
            rows = pl.ds(m * 256, 256)
            x = cols[z].reshape(size, QW)
            main = dot(bm[0, rows], x) + dot(bm[1, rows], x)
            before = dot(bm[2, rows], x[:, 128:]) + dot(bm[3, rows], x[:, 128:])
            after = dot(bm[4, rows], x[:, :128]) + dot(bm[5, rows], x[:, :128])
            high, low = split2(jnp.concatenate([before, main, after], axis=1))
            out = dot(high, tx[0]) + dot(low, tx[0]) + dot(high, tx[1])
            back[z, pl.ds(m * 16, 16)] = out.astype(BF16).reshape(16, ROWS, QW)
            return carry

        lax.fori_loop(0, size // 256, step, 0)

        def send(i, carry):
            peer = lax.rem(p + i, NP)
            pltpu.make_async_remote_copy(
                back.at[z, peer],
                mixed.at[z, p],
                b_send.at[z],
                b_recv.at[z],
                device_id={"plane": peer},
                device_id_type=MESH,
            ).start()
            return carry

        lax.fori_loop(1, NP, send, 0)
        own = pltpu.make_async_copy(back.at[z, p], mixed.at[z, p], b_own.at[z])
        own.start()
        return own

    def perceive(z, own):
        wait_all(mixed.at[z, pl.ds(0, NP - 1)], b_recv.at[z])
        own.wait()

        def widen(i, carry):
            two = mixed[z, pl.ds(i * 2, 2)].reshape(2 * ROWS, QW).astype(F32)
            for k in range(2):
                wide[k, pl.ds(pl.multiple_of(i * 32, 32), 32)] = two[:, k * 128 : (k + 1) * 128]
            return carry

        lax.fori_loop(0, NP // 2, widen, 0, unroll=4)

        def step(n, carry):
            y = n // 2
            xh = lax.rem(n, 2)
            x = jnp.concatenate(
                [
                    wide[l, pl.ds(8 * xh + 4 * k + y, NP, stride=ROWS)]
                    for k in range(2)
                    for l in range(2)
                ],
                axis=1,
            ).astype(BF16)
            b = bias[...]
            hidden = dot(expand[...], x) + jnp.concatenate([b] * 4, axis=1)
            acc[z * 8 + n] = acc[z * 8 + n] + dot(project_ref[...], gelu(hidden).astype(BF16))
            return carry

        lax.fori_loop(0, 8, step, 0, unroll=2)

    start_direct()
    hand_over()
    owns = [convolve(0)]
    own_copy = start_ring()
    owns.append(convolve(1))
    z_step(1)
    z_step(-1)
    owns.append(convolve(2))
    z_step(2)
    own_copy.wait()
    sample(3)
    perceive(0, owns[0])
    sample(0)
    sample(4)
    perceive(1, owns[1])
    sample(-1, 1)
    sample(5)
    perceive(2, owns[2])
    sample(2)
    sample(6)

    def finish(z, carry):
        def turn(n, carry):
            y = n // 2
            xh = lax.rem(n, 2)
            value = acc[z * 8 + n]
            for k in range(BLK // 128):
                rows_out[xh * 4 + k, pl.ds(y, NP, stride=YR)] = value[:, k * 128 : (k + 1) * 128]
            return carry

        lax.fori_loop(0, 8, turn, 0)

        def write(g, carry):
            rows = pl.ds(pl.multiple_of(g * 8, 8), 8)
            two = jnp.concatenate([rows_out[k, rows] for k in range(8)], axis=1)
            out_ref[pl.ds(g * 2, 2), z] = two.reshape(2, YR, XQ * QW)
            return carry

        lax.fori_loop(0, NP // 2, write, 0)
        return carry

    lax.fori_loop(0, ZD, finish, 0)

    for copy in sends:
        copy.wait_send()
    wait_all(pieces.at[pl.ds(0, (KY - 1) * HELD)], y_send.at[0])
    wait_all(pieces.at[near], y_send.at[1])
    wait_all(rows_all.at[pl.ds(0, NS - 1)], f_send)
    for n, dz in enumerate(DIRECT):
        wait_all(stage[dz].at[pl.ds(0, SLOTS - CAP)], d_send.at[n])
    for z in range(ZD):
        wait_all(chunks.at[z, pl.ds(0, NP - 1)], a_send.at[z])
        wait_all(back.at[z, pl.ds(0, NP - 1)], b_send.at[z])


def body(
    features,
    x_taps,
    y_taps,
    expand,
    expand_bias,
    project,
    atlas_tiles,
    footprint,
    block_slot,
    tile_base,
    displacement,
):
    size = NP * ROWS
    hid = expand.shape[0]
    hbm = pl.BlockSpec(memory_space=pltpu.HBM)
    scalars = pl.BlockSpec(memory_space=pltpu.SMEM)
    vmem = pl.BlockSpec(memory_space=pltpu.VMEM)
    dma = pltpu.SemaphoreType.DMA
    added = pl.pallas_call(
        block_kernel,
        out_shape=jax.ShapeDtypeStruct(features.shape, F32),
        in_specs=[
            hbm,
            scalars,
            scalars,
            vmem,
            vmem,
            vmem,
            hbm,
            scalars,
            vmem,
            scalars,
            scalars,
            vmem,
        ],
        out_specs=vmem,
        scratch_shapes=[
            pltpu.VMEM((ZD, NP, YR, XQ * QW), F32),
            pltpu.VMEM((ZD, NP, ROWS, QW), BF16),
            pltpu.VMEM((ZD, NP, ROWS, QW), BF16),
            pltpu.VMEM((ZD, NP, ROWS, QW), BF16),
            pltpu.VMEM((ZD, NP, ROWS, QW), BF16),
            pltpu.VMEM((NS * HELD, 16, 128), BF16),
            pltpu.VMEM((SLOTS, 16, 128), BF16),
            [pltpu.VMEM((KX, SLOTS, 16, 128), BF16) for _ in GROUPS],
            [pltpu.VMEM((SLOTS, KX, 16, 128), BF16) for _ in DIRECT],
            [pltpu.VMEM((KX, HELD, 16, 128), BF16) for _ in DIRECT],
            [pltpu.VMEM((SLOTS, KX, 16, 128), BF16) for _ in DIRECT],
            pltpu.VMEM((NS, 1, SLOTS), jnp.int32),
            pltpu.SMEM((NS, 1, SLOTS), jnp.int32),
            pltpu.VMEM((6, size, size), BF16),
            pltpu.VMEM((2, 2 * QW, QW), BF16),
            pltpu.VMEM((hid, NP), BF16),
            pltpu.VMEM((hid, hid), F32),
            pltpu.VMEM((NB, TX, BLK), F32),
            pltpu.VMEM((NB, TY, BLK), F32),
            pltpu.VMEM((NB, 8, BLK), F32),
            pltpu.VMEM((2, TY, BLK), F32),
            pltpu.VMEM((NB, NP, BLK), F32),
            pltpu.VMEM((2, size, 128), F32),
            pltpu.VMEM((8, NP * YR, 128), F32),
            dma((ZD + 1,)),
            dma((ZD,)),
            dma((ZD,)),
            dma((ZD,)),
            dma((ZD,)),
            dma((ZD,)),
            dma((2,)),
            dma((2,)),
            dma(()),
            dma((39,)),
            dma((39,)),
            dma(()),
            dma(()),
            dma(()),
            dma((len(DIRECT) * KX,)),
            dma((len(DIRECT),)),
            dma((len(DIRECT),)),
        ],
        compiler_params=pltpu.CompilerParams(
            collective_id=0, has_side_effects=True, vmem_limit_bytes=60 * 1024 * 1024
        ),
        cost_estimate=pl.CostEstimate(
            flops=10_000_000_000, bytes_accessed=10_000_000, transcendentals=1_600_000
        ),
    )(
        features,
        x_taps,
        y_taps,
        expand.T,
        expand_bias.reshape(1, hid),
        project,
        atlas_tiles,
        footprint,
        footprint,
        jnp.swapaxes(block_slot, 1, 2),
        jnp.swapaxes(tile_base, 2, 3),
        displacement,
    )
    return features + added


def solution(mesh):
    return jax.shard_map(
        body,
        mesh=mesh,
        in_specs=(
            P(None, "slab", "plane", None),
            P(),
            P(),
            P(),
            P(),
            P(),
            P("slab", None, None),
            P("slab", None),
            P("slab", "plane", None),
            P(None, "slab", "plane", None),
            P(None, "slab", "plane", None),
        ),
        out_specs=P(None, "slab", "plane", None),
        check_vma=False,
    )
```

```python
import functools

import jax
import jax.numpy as jnp
from jax import lax
from jax.experimental import pallas as pl
from jax.experimental.pallas import tpu as pltpu
from jax.sharding import PartitionSpec as P

TZ = 8
TY = 16
TX = 16
BLK = 512
KZ = 8
KX = 4
NP = KX * KZ
NS = 16
KY = NS // 2
CAP = 2
SLOTS = NS * CAP
HELD = 8
ZD = 3
YR = 4
XQ = 4
QW = 256
ROWS = XQ * YR
NB = ZD * YR * 2
RU, RD = 1, 2
GROUPS = tuple(range(-RU, RD + 1))
DIRECT = tuple(range(RD + 1, KZ - RU))
F32 = jnp.float32
BF16 = jnp.bfloat16
MESH = pl.DeviceIdType.MESH


def dot(a, b):
    return jnp.dot(a, b, preferred_element_type=F32)


def split2(value):
    high = value.astype(BF16)
    return high, (value - high.astype(F32)).astype(BF16)


def gelu(a):
    inner = a * (0.7978845608028654 + (0.7978845608028654 * 0.044715) * (a * a))
    half = 0.5 * a
    return half + half * jnp.tanh(inner)


def wait_all(ref, sem):
    pltpu.make_async_copy(ref, ref, sem).wait()


def block_kernel(
    feat_ref,
    xt_ref,
    yt_ref,
    expand_ref,
    bias_ref,
    project_ref,
    atlas_ref,
    fp_ref,
    row_ref,
    slot_ref,
    base_ref,
    disp_ref,
    out_ref,
    feat,
    chunks,
    cols,
    back,
    mixed,
    pieces,
    picked,
    lib,
    straight,
    held,
    stage,
    rows_all,
    wanted,
    bm,
    tx,
    expand,
    bias,
    wx_all,
    wy_all,
    pz_all,
    wzy,
    acc,
    wide,
    rows_out,
    in_sem,
    a_send,
    a_recv,
    b_send,
    b_recv,
    b_own,
    y_send,
    y_recv,
    g_own,
    g_send,
    g_recv,
    f_send,
    f_recv,
    f_local,
    d_load,
    d_send,
    d_recv,
):
    s = lax.axis_index("slab")
    p = lax.axis_index("plane")
    px = p // KZ
    pz = lax.rem(p, KZ)
    hid = project_ref.shape[1]
    size = NP * ROWS
    lib = dict(zip(GROUPS, lib))
    straight, held, stage = (dict(zip(DIRECT, refs)) for refs in (straight, held, stage))
    sy = s // 2
    core = lax.rem(s, 2)
    chip = lambda d: lax.rem(sy + d + KY, KY) * 2 + core
    beside = s + 1 - 2 * core
    mine = pl.ds((core * KY + sy) * HELD, HELD)
    near = pl.ds(core * KY * HELD, KY * HELD)
    far = pl.ds((1 - core) * KY * HELD, KY * HELD)

    barrier = pltpu.get_barrier_semaphore()

    def greet_plane(i, carry):
        pl.semaphore_signal(
            barrier, inc=1, device_id={"plane": lax.rem(p + i, NP)}, device_id_type=MESH
        )
        return carry

    lax.fori_loop(1, NP, greet_plane, 0)

    def greet_slab(i, carry):
        pl.semaphore_signal(
            barrier, inc=1, device_id={"slab": lax.rem(s + i, NS)}, device_id_type=MESH
        )
        return carry

    lax.fori_loop(1, NS, greet_slab, 0)

    loads = [
        pltpu.make_async_copy(feat_ref.at[:, z], feat.at[z], in_sem.at[z]) for z in range(ZD)
    ]
    half = px // 2
    cell = 2 * pz + lax.rem(px, 2)
    atlas_load = pltpu.make_async_copy(
        atlas_ref.at[
            :,
            pl.ds(pl.multiple_of(half * 16, 16), 16),
            pl.ds(pl.multiple_of(cell * 128, 128), 128),
        ],
        pieces.at[mine],
        in_sem.at[ZD],
    )
    atlas_load.start()
    held_loads = []
    for n, dz in enumerate(DIRECT):
        for q in range(KX):
            start = (2 * lax.rem(pz + dz + KZ, KZ) + q % 2) * 128
            held_loads.append(
                pltpu.make_async_copy(
                    atlas_ref.at[
                        :, pl.ds(q // 2 * 16, 16), pl.ds(pl.multiple_of(start, 128), 128)
                    ],
                    held[dz].at[q],
                    d_load.at[n * KX + q],
                )
            )
    for load in loads + held_loads:
        load.start()

    def make_chunks(z):
        loads[z].wait()

        def step(c, carry):
            block = feat[z, c]
            stacked = jnp.concatenate(
                [block[:, q * QW : (q + 1) * QW] for q in range(XQ)], axis=0
            )
            chunks[z, c] = stacked.astype(BF16)
            return carry

        lax.fori_loop(0, NP, step, 0, unroll=4)

    def send_chunks(z):
        def step(i, carry):
            peer = lax.rem(p + i, NP)
            pltpu.make_async_remote_copy(
                chunks.at[z, peer],
                cols.at[z, p],
                a_send.at[z],
                a_recv.at[z],
                device_id={"plane": peer},
                device_id_type=MESH,
            ).start()
            return carry

        lax.fori_loop(1, NP, step, 0)

    for z in range(ZD):
        make_chunks(z)
        cols[z, p] = chunks[z, p]
    def taps_at(index, ref):
        total = jnp.zeros(index.shape, F32)
        for t in range(31):
            total = jnp.where(index == t, ref[p, t], total)
        return total

    def build_rows(m, carry):
        out = lax.broadcasted_iota(jnp.int32, (64, size), 0) + m * 64
        inp = lax.broadcasted_iota(jnp.int32, (64, size), 1)
        row = lambda r: lax.shift_right_logical(r, 4) * 4 + (r & 3)
        quarter = lambda r: lax.shift_right_logical(r, 2) & 3
        weights = taps_at(row(inp) - row(out) + 15, yt_ref)
        for n, shift in enumerate((0, -1, 1)):
            kept = jnp.where(quarter(inp) == quarter(out) + shift, weights, 0.0)
            high, low = split2(kept)
            bm[2 * n, pl.ds(m * 64, 64)] = high
            bm[2 * n + 1, pl.ds(m * 64, 64)] = low
        return carry

    lax.fori_loop(0, size // 64, build_rows, 0)

    def build_x(m, carry):
        k = lax.broadcasted_iota(jnp.int32, (64, QW), 0) + m * 64
        n = lax.broadcasted_iota(jnp.int32, (64, QW), 1)
        high, low = split2(taps_at(k - 128 - n + 15, xt_ref))
        tx[0, pl.ds(m * 64, 64)] = high
        tx[1, pl.ds(m * 64, 64)] = low
        return carry

    lax.fori_loop(0, 8, build_x, 0)

    expand[...] = jnp.transpose(expand_ref[...].astype(F32)).astype(BF16)
    bias[...] = jnp.transpose(jnp.broadcast_to(bias_ref[...], (hid, hid)))

    def tents_of(n, carry):
        z = n // 8
        y = lax.rem(n, 8) // 2
        xh = lax.rem(n, 2)
        lanes = pl.ds(pl.multiple_of(xh * BLK, BLK), BLK)

        def place(axis, cells):
            base = base_ref[axis, z, xh, y].astype(F32)
            return jnp.clip(disp_ref[axis, z, pl.ds(y, 1), lanes] + base, 0.0, cells - 1.0)

        def tent(axis, cells):
            grid = lax.broadcasted_iota(jnp.int32, (cells, BLK), 0).astype(F32)
            return jnp.maximum(0.0, 1.0 - jnp.abs(place(axis, cells) - grid))

        wy_all[n] = tent(1, TY)
        wx_all[n] = tent(2, TX)
        pz_all[n] = jnp.broadcast_to(place(0, TZ), (8, BLK))
        acc[n] = jnp.zeros((NP, BLK), F32)
        return carry

    lax.fori_loop(0, NB, tents_of, 0)

    atlas_load.wait()
    pl.semaphore_wait(barrier, NP - 1 + NS - 1)

    def send_row(i, carry):
        pltpu.make_async_remote_copy(
            row_ref,
            rows_all.at[s],
            f_send,
            f_recv,
            device_id={"slab": lax.rem(s + i, NS)},
            device_id_type=MESH,
        ).start()
        return carry

    lax.fori_loop(1, NS, send_row, 0)
    rows_all[s] = row_ref[...]

    def send_piece(i, carry):
        pltpu.make_async_remote_copy(
            pieces.at[mine],
            pieces.at[mine],
            y_send.at[0],
            y_recv.at[0],
            device_id={"slab": chip(i)},
            device_id_type=MESH,
        ).start()
        return carry

    lax.fori_loop(1, KY, send_piece, 0)
    for z in range(ZD):
        send_chunks(z)

    sends = []

    def pass_on(source, target, device, index):
        copy = pltpu.make_async_remote_copy(
            source,
            target,
            g_send.at[len(sends)],
            g_recv.at[index],
            device_id={"plane": device},
            device_id_type=MESH,
        )
        copy.start()
        sends.append(copy)
        return copy

    at = lambda x, z: lax.rem(x + KX, KX) * KZ + lax.rem(z + KZ, KZ)
    recv = {}
    around = (("r", 1), ("l", -1), ("o", 2))

    def spread(dz, source):
        for n, (way, dx) in enumerate(around):
            recv[way, dz] = pass_on(source, lib[dz].at[px], at(px + dx, pz), 7 + 8 * n + dz + 3)

    def hand_over():
        wait_all(pieces.at[pl.ds(0, (KY - 1) * HELD)], y_recv.at[0])
        pltpu.make_async_remote_copy(
            pieces.at[near],
            pieces.at[near],
            y_send.at[1],
            y_recv.at[1],
            device_id={"slab": beside},
            device_id_type=MESH,
        ).start()

    def start_ring():
        wait_all(pieces.at[far], y_recv.at[1])

        def pick(slot, carry):
            tile = jnp.maximum(fp_ref[0, slot], 0)
            owner = tile // HELD
            place = lax.rem(owner, 2) * KY + owner // 2
            picked[slot] = pieces[place * HELD + lax.rem(tile, HELD)]
            return carry

        lax.fori_loop(0, SLOTS, pick, 0)
        spread(0, picked)
        for dz in GROUPS:
            if dz:
                recv["z", dz] = pass_on(picked, lib[dz].at[px], at(px, pz - dz), dz + 3)
        copy = pltpu.make_async_copy(picked, lib[0].at[px], g_own)
        copy.start()
        return copy

    def start_direct():
        wait_all(rows_all.at[pl.ds(0, NS - 1)], f_recv)
        local = pltpu.make_async_copy(rows_all, wanted, f_local)
        local.start()
        for load in held_loads:
            load.wait()
        local.wait()
        for n, dz in enumerate(DIRECT):

            def fill(j, carry):
                tile = wanted[j // CAP, 0, s * CAP + lax.rem(j, CAP)] - s * HELD
                tile = jnp.clip(tile, 0, HELD - 1)
                for q in range(KX):
                    stage[dz][j, q] = held[dz][q, tile]
                return carry

            lax.fori_loop(0, SLOTS, fill, 0, unroll=2)

            def send(i, carry):
                peer = lax.rem(s + i, NS)
                pltpu.make_async_remote_copy(
                    stage[dz].at[pl.ds(peer * CAP, CAP)],
                    straight[dz].at[pl.ds(s * CAP, CAP)],
                    d_send.at[n],
                    d_recv.at[n],
                    device_id={"slab": peer},
                    device_id_type=MESH,
                ).start()
                return carry

            lax.fori_loop(1, NS, send, 0)
            straight[dz][pl.ds(s * CAP, CAP)] = stage[dz][pl.ds(s * CAP, CAP)]

    def z_step(dz):
        recv["z", dz].wait_recv()
        spread(dz, lib[dz].at[px])

    def sample(*groups):
        for dz in groups:
            if dz in GROUPS:
                for way, _ in around:
                    recv[way, dz].wait_recv()
            else:
                wait_all(straight[dz].at[pl.ds(0, SLOTS - CAP)], d_recv.at[DIRECT.index(dz)])

        def part(dz, q, slot):
            return lib[dz][q, slot] if dz in GROUPS else straight[dz][slot, q]

        indices = [lax.rem(pz + dz + KZ, KZ).astype(F32) for dz in groups]

        def step(n, carry):
            slot = slot_ref[n // 8, lax.rem(n, 2), lax.rem(n, 8) // 2]
            wy, wx, place = wy_all[n], wx_all[n], pz_all[n]
            for g, index in enumerate(indices):
                wz = jnp.maximum(0.0, 1.0 - jnp.abs(place - index))
                wzy[g, 0:8] = wz * wy[0:8]
                wzy[g, 8:16] = wz * wy[8:16]
            interp = jnp.concatenate(
                [
                    (wzy[g, j : j + 1] * wx).astype(BF16)
                    for g in range(len(groups))
                    for j in range(TY)
                ],
                axis=0,
            )
            tile = jnp.concatenate(
                [
                    jnp.concatenate(
                        [part(dz, 2 * h + k, slot) for dz in groups for k in range(2)], axis=1
                    )
                    for h in range(2)
                ],
                axis=0,
            )
            acc[n] = acc[n] + dot(tile, interp)
            return carry

        lax.fori_loop(0, NB, step, 0, unroll=4)

    def convolve(z):
        wait_all(cols.at[z, pl.ds(0, NP - 1)], a_recv.at[z])

        def step(m, carry):
            rows = pl.ds(m * 256, 256)
            x = cols[z].reshape(size, QW)
            main = dot(bm[0, rows], x) + dot(bm[1, rows], x)
            before = dot(bm[2, rows], x[:, 128:]) + dot(bm[3, rows], x[:, 128:])
            after = dot(bm[4, rows], x[:, :128]) + dot(bm[5, rows], x[:, :128])
            high, low = split2(jnp.concatenate([before, main, after], axis=1))
            out = dot(high, tx[0]) + dot(low, tx[0]) + dot(high, tx[1])
            back[z, pl.ds(m * 16, 16)] = out.astype(BF16).reshape(16, ROWS, QW)
            return carry

        lax.fori_loop(0, size // 256, step, 0)

        def send(i, carry):
            peer = lax.rem(p + i, NP)
            pltpu.make_async_remote_copy(
                back.at[z, peer],
                mixed.at[z, p],
                b_send.at[z],
                b_recv.at[z],
                device_id={"plane": peer},
                device_id_type=MESH,
            ).start()
            return carry

        lax.fori_loop(1, NP, send, 0)
        own = pltpu.make_async_copy(back.at[z, p], mixed.at[z, p], b_own.at[z])
        own.start()
        return own

    def perceive(z, own):
        wait_all(mixed.at[z, pl.ds(0, NP - 1)], b_recv.at[z])
        own.wait()

        def widen(i, carry):
            two = mixed[z, pl.ds(i * 2, 2)].reshape(2 * ROWS, QW).astype(F32)
            for k in range(2):
                wide[k, pl.ds(pl.multiple_of(i * 32, 32), 32)] = two[:, k * 128 : (k + 1) * 128]
            return carry

        lax.fori_loop(0, NP // 2, widen, 0, unroll=4)

        def step(n, carry):
            y = n // 2
            xh = lax.rem(n, 2)
            x = jnp.concatenate(
                [
                    wide[l, pl.ds(8 * xh + 4 * k + y, NP, stride=ROWS)]
                    for k in range(2)
                    for l in range(2)
                ],
                axis=1,
            ).astype(BF16)
            b = bias[...]
            hidden = dot(expand[...], x) + jnp.concatenate([b] * 4, axis=1)
            acc[z * 8 + n] = acc[z * 8 + n] + dot(project_ref[...], gelu(hidden).astype(BF16))
            return carry

        lax.fori_loop(0, 8, step, 0, unroll=2)

    start_direct()
    hand_over()
    owns = [convolve(0)]
    own_copy = start_ring()
    owns.append(convolve(1))
    z_step(1)
    z_step(-1)
    owns.append(convolve(2))
    z_step(2)
    own_copy.wait()
    sample(3)
    perceive(0, owns[0])
    sample(0)
    sample(4)
    perceive(1, owns[1])
    sample(-1, 1)
    sample(5)
    perceive(2, owns[2])
    sample(2)
    sample(6)

    def finish(z, carry):
        def turn(n, carry):
            y = n // 2
            xh = lax.rem(n, 2)
            value = acc[z * 8 + n]
            for k in range(BLK // 128):
                rows_out[xh * 4 + k, pl.ds(y, NP, stride=YR)] = value[:, k * 128 : (k + 1) * 128]
            return carry

        lax.fori_loop(0, 8, turn, 0)

        def write(g, carry):
            rows = pl.ds(pl.multiple_of(g * 8, 8), 8)
            two = jnp.concatenate([rows_out[k, rows] for k in range(8)], axis=1)
            two = two.reshape(2, YR, XQ * QW)
            out_ref[pl.ds(g * 2, 2), z] = feat[z, pl.ds(g * 2, 2)] + two
            return carry

        lax.fori_loop(0, NP // 2, write, 0)
        return carry

    lax.fori_loop(0, ZD, finish, 0)

    for copy in sends:
        copy.wait_send()
    wait_all(pieces.at[pl.ds(0, (KY - 1) * HELD)], y_send.at[0])
    wait_all(pieces.at[near], y_send.at[1])
    wait_all(rows_all.at[pl.ds(0, NS - 1)], f_send)
    for n, dz in enumerate(DIRECT):
        wait_all(stage[dz].at[pl.ds(0, SLOTS - CAP)], d_send.at[n])
    for z in range(ZD):
        wait_all(chunks.at[z, pl.ds(0, NP - 1)], a_send.at[z])
        wait_all(back.at[z, pl.ds(0, NP - 1)], b_send.at[z])


def body(
    features,
    x_taps,
    y_taps,
    expand,
    expand_bias,
    project,
    atlas_tiles,
    footprint,
    block_slot,
    tile_base,
    displacement,
):
    size = NP * ROWS
    hid = expand.shape[0]
    hbm = pl.BlockSpec(memory_space=pltpu.HBM)
    scalars = pl.BlockSpec(memory_space=pltpu.SMEM)
    vmem = pl.BlockSpec(memory_space=pltpu.VMEM)
    dma = pltpu.SemaphoreType.DMA
    added = pl.pallas_call(
        block_kernel,
        out_shape=jax.ShapeDtypeStruct(features.shape, F32),
        in_specs=[
            hbm,
            scalars,
            scalars,
            vmem,
            vmem,
            vmem,
            hbm,
            scalars,
            vmem,
            scalars,
            scalars,
            vmem,
        ],
        out_specs=vmem,
        scratch_shapes=[
            pltpu.VMEM((ZD, NP, YR, XQ * QW), F32),
            pltpu.VMEM((ZD, NP, ROWS, QW), BF16),
            pltpu.VMEM((ZD, NP, ROWS, QW), BF16),
            pltpu.VMEM((ZD, NP, ROWS, QW), BF16),
            pltpu.VMEM((ZD, NP, ROWS, QW), BF16),
            pltpu.VMEM((NS * HELD, 16, 128), BF16),
            pltpu.VMEM((SLOTS, 16, 128), BF16),
            [pltpu.VMEM((KX, SLOTS, 16, 128), BF16) for _ in GROUPS],
            [pltpu.VMEM((SLOTS, KX, 16, 128), BF16) for _ in DIRECT],
            [pltpu.VMEM((KX, HELD, 16, 128), BF16) for _ in DIRECT],
            [pltpu.VMEM((SLOTS, KX, 16, 128), BF16) for _ in DIRECT],
            pltpu.VMEM((NS, 1, SLOTS), jnp.int32),
            pltpu.SMEM((NS, 1, SLOTS), jnp.int32),
            pltpu.VMEM((6, size, size), BF16),
            pltpu.VMEM((2, 2 * QW, QW), BF16),
            pltpu.VMEM((hid, NP), BF16),
            pltpu.VMEM((hid, hid), F32),
            pltpu.VMEM((NB, TX, BLK), F32),
            pltpu.VMEM((NB, TY, BLK), F32),
            pltpu.VMEM((NB, 8, BLK), F32),
            pltpu.VMEM((2, TY, BLK), F32),
            pltpu.VMEM((NB, NP, BLK), F32),
            pltpu.VMEM((2, size, 128), F32),
            pltpu.VMEM((8, NP * YR, 128), F32),
            dma((ZD + 1,)),
            dma((ZD,)),
            dma((ZD,)),
            dma((ZD,)),
            dma((ZD,)),
            dma((ZD,)),
            dma((2,)),
            dma((2,)),
            dma(()),
            dma((39,)),
            dma((39,)),
            dma(()),
            dma(()),
            dma(()),
            dma((len(DIRECT) * KX,)),
            dma((len(DIRECT),)),
            dma((len(DIRECT),)),
        ],
        compiler_params=pltpu.CompilerParams(
            collective_id=0, has_side_effects=True, vmem_limit_bytes=60 * 1024 * 1024
        ),
        cost_estimate=pl.CostEstimate(
            flops=10_000_000_000, bytes_accessed=10_000_000, transcendentals=1_600_000
        ),
    )(
        features,
        x_taps,
        y_taps,
        expand.T,
        expand_bias.reshape(1, hid),
        project,
        atlas_tiles,
        footprint,
        footprint,
        jnp.swapaxes(block_slot, 1, 2),
        jnp.swapaxes(tile_base, 2, 3),
        displacement,
    )
    return added


def solution(mesh):
    return jax.shard_map(
        body,
        mesh=mesh,
        in_specs=(
            P(None, "slab", "plane", None),
            P(),
            P(),
            P(),
            P(),
            P(),
            P("slab", None, None),
            P("slab", None),
            P("slab", "plane", None),
            P(None, "slab", "plane", None),
            P(None, "slab", "plane", None),
        ),
        out_specs=P(None, "slab", "plane", None),
        check_vma=False,
    )
```
